512 devices in a mesh: elem: 512 (over z, y, x, core).
Axes of the slice: x: 4, y: 4, z: 16, core: 2. Of those that a mesh axis runs over, the one named last changes fastest.
Arguments:
- right_side: float32 [2048, 320], P('elem'), may hold values from -6 to 6
- diag_blocks: float32 [2048, 320, 320], P('elem')
- face_blocks: float32 [2048, 6, 80, 80], P('elem'), may hold values from -0.15625 to 0.15625
- neighbours: int32 [2048, 6], P('elem'), may hold values from -1 to 2047, as said below
Outputs:
- basis_q: float32 [2048, 5, 320], P('elem')
- r_factor: float32 [5, 5], replicated
- update: float32 [2048, 320], P('elem')
The draws below stay inside these ranges and needn't reach their ends.
Inputs may be any that keep to these rules, and one draw needn't show every extreme that they name: Neighbours are mutual: if neighbours[e, f] = g >= 0 then neighbours[g, f xor 1] = e. Element e lies on device e // 4; across faces 0 and 1 the neighbour lies on the device before and after it, across faces 2 to 5 on the same device. Facing nodes of the two elements match in order.
All inputs are finite; a program needn't handle non-finite values.
Results may differ from the reference program's by a relative error of at most 0.0034.
Values sent between devices are 32-bit elements; how exact they have to be, the bound alone decides.
A program may use at most 64 MiB of HBM per device.

```python
import jax
import jax.numpy as jnp
from jax import lax

FIELDS = 5
ORDER = 3
NODES = 64
FACE = 16
POWERS = 4
BASIS = 5
ELEM_DEV = 4
ELEMS = 2048
N_ELEM = 512


def draw_diag_blocks(key, part):
    key = jax.random.fold_in(key, 3)
    width = FIELDS * NODES
    noise = jax.random.normal(key, (ELEMS, width, width), jnp.float32)
    return jnp.eye(width, dtype=jnp.float32)[None] + 0.2 / width ** 0.5 * noise


def draw_neighbours(key, part):
    key = jax.random.fold_in(key, 11)
    keys = jax.random.split(key, N_ELEM)
    perms = jax.vmap(lambda single: jax.random.permutation(single, ELEM_DEV))(keys).astype(jnp.int32)
    places = jnp.argsort(perms, axis=1).astype(jnp.int32)
    device = jnp.arange(N_ELEM, dtype=jnp.int32)[:, None] + jnp.zeros((1, ELEM_DEV), jnp.int32)
    rows_y = places // 2
    level = places % 2
    span_y = ELEM_DEV // 2
    before = jnp.clip(device - 1, 0, N_ELEM - 1)
    after = jnp.clip(device + 1, 0, N_ELEM - 1)
    minus_x = jnp.where(device > 0, before * ELEM_DEV + perms[before, places], -1)
    plus_x = jnp.where(device < N_ELEM - 1, after * ELEM_DEV + perms[after, places], -1)
    minus_y = jnp.where(rows_y > 0, device * ELEM_DEV + perms[device, jnp.clip(places - 2, 0, ELEM_DEV - 1)], -1)
    plus_y = jnp.where(rows_y < span_y - 1, device * ELEM_DEV + perms[device, jnp.clip(places + 2, 0, ELEM_DEV - 1)], -1)
    minus_z = jnp.where(level == 1, device * ELEM_DEV + perms[device, jnp.clip(places - 1, 0, ELEM_DEV - 1)], -1)
    plus_z = jnp.where(level == 0, device * ELEM_DEV + perms[device, jnp.clip(places + 1, 0, ELEM_DEV - 1)], -1)
    table = jnp.stack([minus_x, plus_x, minus_y, plus_y, minus_z, plus_z], -1)
    return table.reshape(N_ELEM * ELEM_DEV, 6).astype(jnp.int32)


def shard_levels(stream_key, dims, pieces, smallest, largest):
    def one(dim, shards_of):
        draws = jax.random.uniform(jax.random.fold_in(jax.random.fold_in(stream_key, 6), dim), (shards_of,), jnp.float32, smallest / len(pieces), largest / len(pieces))
        return jnp.repeat(jnp.exp(draws), dims[dim] // shards_of).reshape((-1,) + (1,) * (len(dims) - dim - 1))

    loudness = one(*pieces[0])
    for cut in pieces[1:]:
        loudness = loudness * one(*cut)
    return loudness


def scatter_about(stream_key, extent, scale, reach, cuts=(), kind=jnp.bfloat16):
    drawn = jax.random.normal(stream_key, extent, jnp.float32) * scale
    if len(cuts) > 0:
        drawn = shard_levels(stream_key, extent, cuts, -0.22, 0.18) * drawn
    return jnp.clip(drawn, min=-reach, max=reach).astype(kind)


def setup_inputs(seed: int = 0) -> dict:
    key_of = jax.random.split(jax.random.key(seed), 5)
    return {
        "right_side": scatter_about(key_of[0], (ELEMS, FIELDS * NODES), 1.0, 6.0, ((0, 512),), jnp.float32),
        "diag_blocks": draw_diag_blocks(jax.random.fold_in(key_of[4], 71), 0),
        "face_blocks": scatter_about(key_of[2], (ELEMS, 6, FIELDS * FACE, FIELDS * FACE), (16 * FIELDS * FACE) ** -0.5, 0.15625, ((0, 512),), jnp.float32),
        "neighbours": draw_neighbours(jax.random.fold_in(key_of[4], 71), 0),
    }


OPPOSITE = (1, 0, 3, 2, 5, 4)

def face_traces(cube):
    count = cube.shape[0]
    sides = [cube[:, :, 0], cube[:, :, ORDER], cube[:, :, :, 0], cube[:, :, :, ORDER], cube[:, :, :, :, 0], cube[:, :, :, :, ORDER]]
    return [side.reshape(count, -1) for side in sides]

def add_faces(cube, contrib):
    count = cube.shape[0]
    shape = (count, FIELDS, ORDER + 1, ORDER + 1)
    cube = cube.at[:, :, 0].add(contrib[:, 0].reshape(shape))
    cube = cube.at[:, :, ORDER].add(contrib[:, 1].reshape(shape))
    cube = cube.at[:, :, :, 0].add(contrib[:, 2].reshape(shape))
    cube = cube.at[:, :, :, ORDER].add(contrib[:, 3].reshape(shape))
    cube = cube.at[:, :, :, :, 0].add(contrib[:, 4].reshape(shape))
    cube = cube.at[:, :, :, :, ORDER].add(contrib[:, 5].reshape(shape))
    return cube

def operate(vector, diag_blocks, face_blocks, neighbours):
    count = vector.shape[0]
    cube = vector.reshape(count, FIELDS, ORDER + 1, ORDER + 1, ORDER + 1)
    traces = face_traces(cube)
    valid = neighbours >= 0
    safe = jnp.where(valid, neighbours, 0)
    incoming = jnp.stack([jnp.where(valid[:, f, None], traces[OPPOSITE[f]][safe[:, f]], jnp.float32(0.0)) for f in range(6)], 1)
    contrib = jnp.einsum('efab,efb->efa', face_blocks, incoming, precision=lax.Precision.HIGHEST)
    own = jnp.einsum('eab,eb->ea', diag_blocks, vector, precision=lax.Precision.HIGHEST)
    return add_faces(own.reshape(cube.shape), contrib).reshape(count, -1)

def small_solve(r_factor):
    square = r_factor[:POWERS, :POWERS]
    tail = r_factor[:, 1:]
    hess = jax.scipy.linalg.solve_triangular(square.T, tail.T, lower=True).T
    normal = jnp.dot(hess.T, hess, precision=lax.Precision.HIGHEST)
    target = r_factor[0, 0] * hess[0, :]
    lower = jnp.linalg.cholesky(normal)
    middle = jax.scipy.linalg.solve_triangular(lower, target, lower=True)
    solved = jax.scipy.linalg.solve_triangular(lower.T, middle, lower=False)
    return jax.scipy.linalg.solve_triangular(square, solved, lower=False)

def reference(right_side, diag_blocks, face_blocks, neighbours):
    vector = right_side
    basis = [vector]
    for power in range(POWERS):
        vector = operate(vector, diag_blocks, face_blocks, neighbours)
        basis.append(vector)
    stacked = jnp.stack(basis, 1)
    count, width = right_side.shape
    columns = stacked.transpose(0, 2, 1).reshape(-1, BASIS)
    q_matrix, r_matrix = jnp.linalg.qr(columns)
    signs = jnp.sign(jnp.diagonal(r_matrix))
    r_matrix = r_matrix * signs[:, None]
    q_matrix = q_matrix * signs[None, :]
    basis_q = q_matrix.reshape(count, width, BASIS).transpose(0, 2, 1)
    coeffs = small_solve(r_matrix)
    update = jnp.einsum('k,ekm->em', coeffs, stacked[:, :POWERS], precision=lax.Precision.HIGHEST)
    return (basis_q, r_matrix, update)
```

```python
import jax
import jax.numpy as jnp
from jax import lax
from jax.experimental import pallas as pl
from jax.experimental.pallas import tpu as pltpu
from jax.sharding import PartitionSpec as P

POWERS = 4
BASIS = 5
ELEM_DEV = 4
WIDTH = 320
FACE_WIDTH = 80
N_DEV = 512
PLANE = 32
N_Z = 16
F32 = jnp.float32
MESH = pl.DeviceIdType.MESH


def iota(shape, dim):
    return lax.broadcasted_iota(jnp.int32, shape, dim)


def two_sum(a, b):
    s = a + b
    t = s - a
    return s, (a - (s - t)) + (b - t)


def fast_two_sum(a, b):
    s = a + b
    return s, b - (s - a)


def split(a):
    c = a * 4097.0
    high = c - (c - a)
    return high, a - high


def two_prod(a, b):
    p = a * b
    ah, al = split(a)
    bh, bl = split(b)
    return p, ((ah * bh - p) + ah * bl + al * bh) + al * bl


def trace_tiles(tiles):
    lane = iota((8, 128), 1)
    within, field_odd = lane % 16, (lane // 16) % 2
    u, w = within // 4, within % 4
    offsets = [
        4 * u + w,
        48 + 4 * u + w,
        16 * u + w,
        16 * u + 12 + w,
        16 * u + 4 * w,
        16 * u + 4 * w + 3,
    ]
    out = []
    for offset in offsets:
        index = field_odd * 64 + offset
        got = [jnp.take_along_axis(tile, index, axis=1) for tile in tiles]
        out.append(jnp.where(lane < 32, got[0], jnp.where(lane < 64, got[1], got[2])))
    return out


def face_lane(face, rows, first):
    a = iota((rows, 128), 0) + first
    field_odd, within = (a // 16) % 2, a % 16
    u, w = within // 4, within % 4
    offset = [
        4 * u + w,
        48 + 4 * u + w,
        16 * u + w,
        16 * u + 12 + w,
        16 * u + 4 * w,
        16 * u + 4 * w + 3,
    ][face]
    return field_odd * 64 + offset


def fold(placed):
    return jnp.sum(placed.reshape(-1, 8, 128), axis=0)


def place_element(column):
    out = []
    for tile in range(3):
        rows = min(128, WIDTH - 128 * tile)
        part = jnp.broadcast_to(column[128 * tile : 128 * tile + rows], (rows, 128))
        out.append(fold(jnp.where(iota((rows, 128), 0) == iota((rows, 128), 1), part, 0.0)))
    return out


def place_face(face, column):
    out = []
    for tile in range(3):
        rows = min(32, FACE_WIDTH - 32 * tile)
        part = jnp.broadcast_to(column[32 * tile : 32 * tile + rows], (rows, 128))
        out.append(fold(jnp.where(face_lane(face, rows, 32 * tile) == iota((rows, 128), 1), part, 0.0)))
    return out


def place_trace(column):
    shape = (FACE_WIDTH, 128)
    part = jnp.broadcast_to(column, shape)
    return jnp.sum(jnp.where(iota(shape, 0) == iota(shape, 1), part, 0.0), axis=0, keepdims=True)


def add_all(left, right):
    return [a + b for a, b in zip(left, right)]


def matvec(matrix, row):
    return jnp.sum(matrix * row, axis=1, keepdims=True)


def gram_column(basis, k):
    chains = []
    for tile in range(3):
        total, low = None, None
        for e in range(ELEM_DEV):
            x = basis[e, :, 128 * tile : 128 * tile + 128]
            b = jnp.broadcast_to(basis[e, k : k + 1, 128 * tile : 128 * tile + 128], (8, 128))
            p, err = two_prod(x, b)
            if total is None:
                total, low = p, err
            else:
                total, more = two_sum(total, p)
                low = low + (err + more)
        chains.append((total, low))
    total, low = chains[0]
    for other, other_low in chains[1:]:
        total, more = two_sum(total, other)
        low = low + (other_low + more)
    for shift in (64, 32, 16, 8, 4, 2, 1):
        other, other_low = pltpu.roll(total, shift, 1), pltpu.roll(low, shift, 1)
        total, more = two_sum(total, other)
        low = (low + other_low) + more
    return total, low


def pack(message, k, pair):
    lane = iota((8, 128), 1)
    message = jnp.where(lane == k, pair[0], message)
    return jnp.where(lane == 8 + k, pair[1], message)


def sum_messages(tiles):
    chains = []
    for start in range(4):
        mine = tiles[start::4]
        total, low = mine[0], jnp.zeros((8, 128), F32)
        for tile in mine[1:]:
            total, more = two_sum(total, tile)
            low = low + more
        chains.append((total, low))
    while len(chains) > 1:
        merged = []
        for a, b in zip(chains[::2], chains[1::2]):
            total, more = two_sum(a[0], b[0])
            merged.append((total, (a[1] + b[1]) + more))
        chains = merged
    total, low = chains[0]
    return fast_two_sum(total, low + pltpu.roll(total, 120, 1))


def repack(high, low):
    return jnp.where(iota((8, 128), 1) < 8, high, pltpu.roll(low, 8, 1))


def solve(high, low):
    def spread(tile, i, k):
        return jnp.broadcast_to(tile[i : i + 1, k : k + 1], (8, 128))

    g = {(i, k): (spread(high, i, k), spread(low, i, k)) for i in range(BASIS) for k in range(i, BASIS)}
    factors, inverse, r = {}, [], {}
    for j in range(BASIS):
        d, d_low = g[j, j]
        root = lax.rsqrt(d)
        root = root * (1.5 - 0.5 * d * root * root)
        inverse.append(root)
        for k in range(j, BASIS):
            r[j, k] = g[j, k][0] * root
        if j == BASIS - 1:
            break
        recip = 1.0 / d
        ls = {}
        for i in range(j + 1, BASIS):
            t, t_low = g[j, i]
            first = t * recip
            p, err = two_prod(first, d)
            rest = (((t - p) - err) + t_low) - first * d_low
            ls[i] = fast_two_sum(first, rest * recip)
            factors[i, j] = ls[i][0]
        for i in range(j + 1, BASIS):
            for k in range(i, BASIS):
                t, t_low = g[j, k]
                p, err = two_prod(ls[i][0], t)
                err = err + (ls[i][0] * t_low + ls[i][1] * t)
                total, more = two_sum(g[i, k][0], -p)
                g[i, k] = fast_two_sum(total, more + (g[i, k][1] - err))
    h = {}
    for j in range(POWERS):
        for i in range(j + 2):
            value = r[i, j + 1]
            for m in range(max(i - 1, 0), j):
                value = value - h[i, m] * r[m, j]
            h[i, j] = value * inverse[j]
    normal = {}
    for a in range(POWERS):
        for b in range(a, POWERS):
            value = h[0, a] * h[0, b]
            for i in range(1, a + 2):
                value = value + h[i, a] * h[i, b]
            normal[a, b] = value
    target = [r[0, 0] * h[0, a] for a in range(POWERS)]
    lower, recips = {}, []
    for j in range(POWERS):
        recips.append(1.0 / normal[j, j])
        for i in range(j + 1, POWERS):
            lower[i, j] = normal[j, i] * recips[j]
        for i in range(j + 1, POWERS):
            target[i] = target[i] - lower[i, j] * target[j]
            for k in range(i, POWERS):
                normal[i, k] = normal[i, k] - lower[i, j] * normal[j, k]
    y = [target[j] * recips[j] for j in range(POWERS)]
    for j in range(POWERS - 1, -1, -1):
        for i in range(j + 1, POWERS):
            y[j] = y[j] - lower[i, j] * y[i]
    return factors, r, inverse, y


def kernel(
    nb_ref, rhs_ref, diag_hbm, face_hbm,
    q_ref, r_ref, up_ref,
    diag, face, basis, rows, traces, out_x, in_a, in_b, in_c, in_d, far, message, got_plane, got_z,
    load_sem, far_send, far_recv, x_send, x_recv, p_send, p_recv, z_send, z_recv,
):
    in_x = ((in_a, in_b), (in_c, in_d))
    me = lax.axis_index("elem")
    place, z, core = me % PLANE, me // PLANE, me % 2
    plane0 = me - place

    loads = [
        pltpu.make_async_copy(diag_hbm, diag, load_sem.at[0]),
        pltpu.make_async_copy(face_hbm, face, load_sem.at[1]),
    ]
    for load in loads:
        load.start()

    barrier = pltpu.get_barrier_semaphore()

    def greet(device):
        pl.semaphore_signal(barrier, inc=1, device_id=(device,), device_id_type=MESH)

    for d in range(1, N_Z):
        greet(((z + d) % N_Z) * PLANE + place - core + 1)

    @pl.when(core == 1)
    def _():
        for d in range(1, PLANE):
            greet(plane0 + (place + d) % PLANE)

        @pl.when(jnp.logical_and(place == PLANE - 1, me < N_DEV - 1))
        def _():
            greet(me + 1)

    @pl.when(core == 0)
    def _():
        greet(me + 1)

        @pl.when(me > 0)
        def _():
            greet(me - 1)

    basis[...] = jnp.zeros(basis.shape, F32)
    rows[...] = jnp.zeros(rows.shape, F32)
    rows[0:ELEM_DEV, 0:WIDTH] = rhs_ref[...]

    def store_row(k, e, tiles):
        for t in range(3):
            lanes = min(128, WIDTH - 128 * t)
            row = jnp.sum(tiles[t], axis=0, keepdims=True)[:, :lanes]
            basis[e, k : k + 1, 128 * t : 128 * t + lanes] = row
            rows[e : e + 1, 128 * t : 128 * t + lanes] = row

    def make_traces():
        got = trace_tiles([rows[:, 128 * t : 128 * t + 128] for t in range(3)])
        for f in range(6):
            traces[f] = got[f]

    for e in range(ELEM_DEV):
        basis[e, 0:1, 0:WIDTH] = rhs_ref[e : e + 1, :]
    make_traces()

    def x_traces(tiles):
        got = trace_tiles(tiles)
        return got[0], got[1]

    def send_x(step, kind):
        for side in range(2):
            @pl.when(me > 0 if side == 0 else me < N_DEV - 1)
            def _():
                x_copy(step, kind, side).start()

    def x_copy(step, kind, side):
        return pltpu.make_async_remote_copy(
            src_ref=out_x.at[step, kind, side],
            dst_ref=in_x[step][kind].at[1 - side],
            send_sem=x_send.at[step, kind, side],
            recv_sem=x_recv.at[step, kind, 1 - side],
            device_id=(me - 1 if side == 0 else me + 1,),
            device_id_type=MESH,
        )

    def wait_x(step, kind):
        for side in range(2):
            @pl.when(me < N_DEV - 1 if side == 0 else me > 0)
            def _():
                x_copy(step, kind, side).wait_recv()

    def far_copy(side):
        return pltpu.make_async_remote_copy(
            src_ref=face.at[:, side],
            dst_ref=far.at[1 - side],
            send_sem=far_send.at[side],
            recv_sem=far_recv.at[1 - side],
            device_id=(me - 1 if side == 0 else me + 1,),
            device_id_type=MESH,
        )

    heard = jnp.where(
        core == 1,
        (N_Z - 1) * 2 + 15 + 2 - jnp.where(me == N_DEV - 1, 1, 0),
        16 + jnp.where(jnp.logical_and(place == 0, me > 0), 1, 0),
    )
    pl.semaphore_wait(barrier, heard)

    out_x[0, 0, 0] = traces[0]
    out_x[0, 0, 1] = traces[1]
    send_x(0, 0)
    loads[1].wait()
    for side in range(2):
        @pl.when(me > 0 if side == 0 else me < N_DEV - 1)
        def _():
            far_copy(side).start()
    loads[0].wait()

    base = me * ELEM_DEV

    def link(e, f):
        wanted = nb_ref[e, f]
        first = base + (-ELEM_DEV if f == 0 else ELEM_DEV if f == 1 else 0)
        return wanted >= 0, jnp.clip(wanted - first, 0, ELEM_DEV - 1)

    links = [[link(e, f) for f in range(6)] for e in range(ELEM_DEV)]

    def own_part(out):
        for e in range(ELEM_DEV):
            total = place_element(matvec(diag[e], rows[e : e + 1, 0:WIDTH]))
            for f in range(2, 6):
                valid, index = links[e][f]
                row = jnp.where(valid, traces[f ^ 1, pl.ds(index, 1), :], 0.0)
                total = add_all(total, place_face(f, matvec(face[e, f], row[:, 0:FACE_WIDTH])))
            out.append(total)

    def x_part(e, across):
        total = None
        for f in range(2):
            part = place_face(f, matvec(face[e, f], across[f][:, 0:FACE_WIDTH]))
            total = part if total is None else add_all(total, part)
        return total

    def received(step, kind, e, f):
        valid, index = links[e][f]
        return valid, in_x[step][kind][f, pl.ds(index, 1), :]

    grams = {}
    for step in range(2):
        k = 2 * step
        own = []
        own_part(own)
        sums = [
            jnp.concatenate([jnp.sum(own[e][t], axis=0, keepdims=True) for e in range(ELEM_DEV)] * 2, axis=0)
            for t in range(3)
        ]
        low, high = x_traces(sums)
        out_x[step, 1, 0] = low
        out_x[step, 1, 1] = high
        send_x(step, 1)
        if step == 0:
            for side in range(2):
                @pl.when(me < N_DEV - 1 if side == 0 else me > 0)
                def _():
                    far_copy(side).wait_recv()
        back = []
        for e in range(ELEM_DEV):
            pair = []
            for f in range(2):
                valid, index = links[e][f]
                trace = traces[f, e : e + 1, 0:FACE_WIDTH]
                pair.append(place_trace(matvec(far[f, index], trace)))
            back.append(pair)
        if step == 1:
            for kk in range(3):
                grams[kk] = gram_column(basis, kk)
        wait_x(step, 0)
        for e in range(ELEM_DEV):
            across = []
            for f in range(2):
                valid, row = received(step, 0, e, f)
                across.append(jnp.where(valid, row, 0.0))
            store_row(k + 1, e, add_all(own[e], x_part(e, across)))
        make_traces()
        own = []
        own_part(own)
        wait_x(step, 1)
        for e in range(ELEM_DEV):
            across = []
            for f in range(2):
                valid, row = received(step, 1, e, f)
                across.append(jnp.where(valid, row + back[e][f], 0.0))
            store_row(k + 2, e, add_all(own[e], x_part(e, across)))
        if step == 0:
            make_traces()
            out_x[1, 0, 0] = traces[0]
            out_x[1, 0, 1] = traces[1]
            send_x(1, 0)

    grams[3] = gram_column(basis, 3)
    grams[4] = gram_column(basis, 4)
    packed = jnp.zeros((8, 128), F32)
    for k in range(BASIS):
        packed = pack(packed, k, grams[k])
    message[0] = packed

    def plane_copy(d):
        return pltpu.make_async_remote_copy(
            src_ref=message.at[0],
            dst_ref=got_plane.at[PLANE - d - 1],
            send_sem=p_send,
            recv_sem=p_recv,
            device_id=(plane0 + (place + d) % PLANE,),
            device_id_type=MESH,
        )

    def z_copy(d, to):
        return pltpu.make_async_remote_copy(
            src_ref=message.at[1],
            dst_ref=got_z.at[(N_Z - d) % N_Z],
            send_sem=z_send,
            recv_sem=z_recv,
            device_id=(((z + d) % N_Z) * PLANE + place - core + to,),
            device_id_type=MESH,
        )

    def wait_all(ref, sem):
        pltpu.make_async_copy(ref, ref, sem).wait()

    far_first = sorted(range(1, N_Z), key=lambda d: -min(d, N_Z - d))

    @pl.when(core == 1)
    def _():
        for d in range(2, PLANE, 2):
            plane_copy(d).start()
        wait_all(got_plane, p_recv)
        high, low = sum_messages([message[0]] + [got_plane[i] for i in range(PLANE - 1)])
        message[1] = repack(high, low)
        for d in far_first:
            z_copy(d, 0).start()
        for d in far_first:
            z_copy(d, 1).start()
        z_copy(0, 0).start()
        got_z[0] = message[1]
        wait_all(got_z.at[pl.ds(1, N_Z - 1)], z_recv)

    @pl.when(core == 0)
    def _():
        for d in range(1, PLANE, 2):
            plane_copy(d).start()
        wait_all(got_z, z_recv)

    high, low = sum_messages([got_z[i] for i in range(N_Z)])
    factors, r, inverse, y = solve(high, low)

    sub, lane = iota((8, 128), 0), iota((8, 128), 1)
    r_tile = jnp.zeros((8, 128), F32)
    for (i, k), value in r.items():
        r_tile = jnp.where(jnp.logical_and(sub == i, lane == k), value, r_tile)
    r_ref[...] = r_tile[0:BASIS, 0:BASIS]
    columns = []
    for j in range(BASIS - 1):
        column = jnp.zeros((8, 128), F32)
        for i in range(j + 1, BASIS):
            column = jnp.where(sub == i, factors[i, j], column)
        columns.append(column)
    scale, weight = jnp.zeros((8, 128), F32), jnp.zeros((8, 128), F32)
    for j in range(BASIS):
        scale = jnp.where(sub == j, inverse[j], scale)
        if j < POWERS:
            weight = jnp.where(sub == j, y[j], weight)
    for e in range(ELEM_DEV):
        for t in range(3):
            lanes = min(128, WIDTH - 128 * t)
            x = basis[e, :, 128 * t : 128 * t + 128]
            for j in range(BASIS - 1):
                x = x - columns[j] * x[j : j + 1, :]
            x = x * scale
            q_ref[e, :, 128 * t : 128 * t + lanes] = x[0:BASIS, 0:lanes]
            update = jnp.sum(x * weight, axis=0, keepdims=True)
            up_ref[e : e + 1, 128 * t : 128 * t + lanes] = update[:, 0:lanes]

    for side in range(2):
        @pl.when(me > 0 if side == 0 else me < N_DEV - 1)
        def _():
            far_copy(side).wait_send()
            for step in range(2):
                for kind in range(2):
                    x_copy(step, kind, side).wait_send()

    @pl.when(core == 1)
    def _():
        wait_all(got_plane.at[pl.ds(0, 15)], p_send)
        wait_all(got_plane.at[pl.ds(0, 2 * N_Z - 1)], z_send)

    @pl.when(core == 0)
    def _():
        wait_all(got_plane.at[pl.ds(0, 16)], p_send)


def body(right_side, diag_blocks, face_blocks, neighbours):
    any_space = pl.BlockSpec(memory_space=pl.ANY)
    vmem = pl.BlockSpec(memory_space=pltpu.VMEM)
    tile = (8, 128)
    return pl.pallas_call(
        kernel,
        out_shape=(
            jax.ShapeDtypeStruct((ELEM_DEV, BASIS, WIDTH), F32),
            jax.ShapeDtypeStruct((BASIS, BASIS), F32),
            jax.ShapeDtypeStruct((ELEM_DEV, WIDTH), F32),
        ),
        in_specs=[pl.BlockSpec(memory_space=pltpu.SMEM), vmem, any_space, any_space],
        out_specs=(vmem, vmem, vmem),
        scratch_shapes=[
            pltpu.VMEM((ELEM_DEV, WIDTH, WIDTH), F32),
            pltpu.VMEM((ELEM_DEV, 6, FACE_WIDTH, FACE_WIDTH), F32),
            pltpu.VMEM((ELEM_DEV, 8, 384), F32),
            pltpu.VMEM((8, 384), F32),
            pltpu.VMEM((6,) + tile, F32),
            pltpu.VMEM((2, 2, 2) + tile, F32),
            pltpu.VMEM((2,) + tile, F32),
            pltpu.VMEM((2,) + tile, F32),
            pltpu.VMEM((2,) + tile, F32),
            pltpu.VMEM((2,) + tile, F32),
            pltpu.VMEM((2, ELEM_DEV, FACE_WIDTH, FACE_WIDTH), F32),
            pltpu.VMEM((2,) + tile, F32),
            pltpu.VMEM((PLANE - 1,) + tile, F32),
            pltpu.VMEM((N_Z,) + tile, F32),
            pltpu.SemaphoreType.DMA((2,)),
            pltpu.SemaphoreType.DMA((2,)),
            pltpu.SemaphoreType.DMA((2,)),
            pltpu.SemaphoreType.DMA((2, 2, 2)),
            pltpu.SemaphoreType.DMA((2, 2, 2)),
            pltpu.SemaphoreType.DMA,
            pltpu.SemaphoreType.DMA,
            pltpu.SemaphoreType.DMA,
            pltpu.SemaphoreType.DMA,
        ],
        compiler_params=pltpu.CompilerParams(
            collective_id=0, has_side_effects=True, vmem_limit_bytes=24 * 2**20
        ),
    )(neighbours, right_side, diag_blocks, face_blocks)


def solution(mesh):
    in_specs = (
        P("elem", None),
        P("elem", None, None),
        P("elem", None, None, None),
        P("elem", None),
    )
    out_specs = (P("elem", None, None), P(), P("elem", None))
    return jax.shard_map(body, mesh=mesh, in_specs=in_specs, out_specs=out_specs, check_vma=False)
```

```python
import jax
import jax.numpy as jnp
from jax import lax
from jax.experimental import pallas as pl
from jax.experimental.pallas import tpu as pltpu
from jax.sharding import PartitionSpec as P

POWERS = 4
BASIS = 5
ELEM_DEV = 4
WIDTH = 320
FACE_WIDTH = 80
N_DEV = 512
PLANE = 32
N_Z = 16
F32 = jnp.float32
MESH = pl.DeviceIdType.MESH


def iota(shape, dim):
    return lax.broadcasted_iota(jnp.int32, shape, dim)


def two_sum(a, b):
    s = a + b
    t = s - a
    return s, (a - (s - t)) + (b - t)


def fast_two_sum(a, b):
    s = a + b
    return s, b - (s - a)


def split(a):
    c = a * 4097.0
    high = c - (c - a)
    return high, a - high


def two_prod(a, b):
    p = a * b
    ah, al = split(a)
    bh, bl = split(b)
    return p, ((ah * bh - p) + ah * bl + al * bh) + al * bl


def trace_tiles(tiles):
    lane = iota((8, 128), 1)
    within, field_odd = lane % 16, (lane // 16) % 2
    u, w = within // 4, within % 4
    offsets = [
        4 * u + w,
        48 + 4 * u + w,
        16 * u + w,
        16 * u + 12 + w,
        16 * u + 4 * w,
        16 * u + 4 * w + 3,
    ]
    out = []
    for offset in offsets:
        index = field_odd * 64 + offset
        got = [jnp.take_along_axis(tile, index, axis=1) for tile in tiles]
        out.append(jnp.where(lane < 32, got[0], jnp.where(lane < 64, got[1], got[2])))
    return out


def face_lane(face, rows, first):
    a = iota((rows, 128), 0) + first
    field_odd, within = (a // 16) % 2, a % 16
    u, w = within // 4, within % 4
    offset = [
        4 * u + w,
        48 + 4 * u + w,
        16 * u + w,
        16 * u + 12 + w,
        16 * u + 4 * w,
        16 * u + 4 * w + 3,
    ][face]
    return field_odd * 64 + offset


def fold(placed):
    return jnp.sum(placed.reshape(-1, 8, 128), axis=0)


def place_element(column):
    out = []
    for tile in range(3):
        rows = min(128, WIDTH - 128 * tile)
        part = jnp.broadcast_to(column[128 * tile : 128 * tile + rows], (rows, 128))
        out.append(fold(jnp.where(iota((rows, 128), 0) == iota((rows, 128), 1), part, 0.0)))
    return out


def place_face(face, column):
    out = []
    for tile in range(3):
        rows = min(32, FACE_WIDTH - 32 * tile)
        part = jnp.broadcast_to(column[32 * tile : 32 * tile + rows], (rows, 128))
        out.append(fold(jnp.where(face_lane(face, rows, 32 * tile) == iota((rows, 128), 1), part, 0.0)))
    return out


def place_trace(column):
    shape = (FACE_WIDTH, 128)
    part = jnp.broadcast_to(column, shape)
    return jnp.sum(jnp.where(iota(shape, 0) == iota(shape, 1), part, 0.0), axis=0, keepdims=True)


def add_all(left, right):
    return [a + b for a, b in zip(left, right)]


def matvec(matrix, row):
    return jnp.sum(matrix * row, axis=1, keepdims=True)


def gram_column(basis, k):
    chains = []
    for tile in range(3):
        total, low = None, None
        for e in range(ELEM_DEV):
            x = basis[e, :, 128 * tile : 128 * tile + 128]
            b = jnp.broadcast_to(basis[e, k : k + 1, 128 * tile : 128 * tile + 128], (8, 128))
            p, err = two_prod(x, b)
            if total is None:
                total, low = p, err
            else:
                total, more = two_sum(total, p)
                low = low + (err + more)
        chains.append((total, low))
    total, low = chains[0]
    for other, other_low in chains[1:]:
        total, more = two_sum(total, other)
        low = low + (other_low + more)
    for shift in (64, 32, 16, 8, 4, 2, 1):
        other, other_low = pltpu.roll(total, shift, 1), pltpu.roll(low, shift, 1)
        total, more = two_sum(total, other)
        low = (low + other_low) + more
    return total, low


def pack(message, k, pair):
    lane = iota((8, 128), 1)
    message = jnp.where(lane == k, pair[0], message)
    return jnp.where(lane == 8 + k, pair[1], message)


def sum_messages(tiles):
    chains = []
    for start in range(4):
        mine = tiles[start::4]
        total, low = mine[0], jnp.zeros((8, 128), F32)
        for tile in mine[1:]:
            total, more = two_sum(total, tile)
            low = low + more
        chains.append((total, low))
    while len(chains) > 1:
        merged = []
        for a, b in zip(chains[::2], chains[1::2]):
            total, more = two_sum(a[0], b[0])
            merged.append((total, (a[1] + b[1]) + more))
        chains = merged
    total, low = chains[0]
    return fast_two_sum(total, low + pltpu.roll(total, 120, 1))


def repack(high, low):
    return jnp.where(iota((8, 128), 1) < 8, high, pltpu.roll(low, 8, 1))


def solve(high, low):
    def spread(tile, i, k):
        return jnp.broadcast_to(tile[i : i + 1, k : k + 1], (8, 128))

    g = {(i, k): (spread(high, i, k), spread(low, i, k)) for i in range(BASIS) for k in range(i, BASIS)}
    factors, inverse, r = {}, [], {}
    for j in range(BASIS):
        d, d_low = g[j, j]
        root = lax.rsqrt(d)
        root = root * (1.5 - 0.5 * d * root * root)
        inverse.append(root)
        for k in range(j, BASIS):
            r[j, k] = g[j, k][0] * root
        if j == BASIS - 1:
            break
        recip = 1.0 / d
        ls = {}
        for i in range(j + 1, BASIS):
            t, t_low = g[j, i]
            first = t * recip
            p, err = two_prod(first, d)
            rest = (((t - p) - err) + t_low) - first * d_low
            ls[i] = fast_two_sum(first, rest * recip)
            factors[i, j] = ls[i][0]
        for i in range(j + 1, BASIS):
            for k in range(i, BASIS):
                t, t_low = g[j, k]
                p, err = two_prod(ls[i][0], t)
                err = err + (ls[i][0] * t_low + ls[i][1] * t)
                total, more = two_sum(g[i, k][0], -p)
                g[i, k] = fast_two_sum(total, more + (g[i, k][1] - err))
    h = {}
    for j in range(POWERS):
        for i in range(j + 2):
            value = r[i, j + 1]
            for m in range(max(i - 1, 0), j):
                value = value - h[i, m] * r[m, j]
            h[i, j] = value * inverse[j]
    normal = {}
    for a in range(POWERS):
        for b in range(a, POWERS):
            value = h[0, a] * h[0, b]
            for i in range(1, a + 2):
                value = value + h[i, a] * h[i, b]
            normal[a, b] = value
    target = [r[0, 0] * h[0, a] for a in range(POWERS)]
    lower, recips = {}, []
    for j in range(POWERS):
        recips.append(1.0 / normal[j, j])
        for i in range(j + 1, POWERS):
            lower[i, j] = normal[j, i] * recips[j]
        for i in range(j + 1, POWERS):
            target[i] = target[i] - lower[i, j] * target[j]
            for k in range(i, POWERS):
                normal[i, k] = normal[i, k] - lower[i, j] * normal[j, k]
    y = [target[j] * recips[j] for j in range(POWERS)]
    for j in range(POWERS - 1, -1, -1):
        for i in range(j + 1, POWERS):
            y[j] = y[j] - lower[i, j] * y[i]
    return factors, r, inverse, y


def kernel(
    nb_hbm, rhs_hbm, diag_hbm, face_hbm,
    basis_hbm, gram_hbm,
    nb_ref, rhs_ref, diag, face, basis, gram, rows, traces, out_x, in_a, in_b, in_c, in_d, far, message, got_plane, got_z,
    load_sem, far_send, far_recv, x_send, x_recv, p_send, p_recv, z_send, z_recv, ready,
):
    in_x = ((in_a, in_b), (in_c, in_d))
    me = lax.axis_index("elem")
    place, z, core = me % PLANE, me // PLANE, me % 2
    plane0 = me - place

    stores = [
        pltpu.make_async_copy(basis, basis_hbm, load_sem.at[4]),
        pltpu.make_async_copy(gram, gram_hbm, load_sem.at[5]),
    ]
    loads = [
        pltpu.make_async_copy(rhs_hbm, rhs_ref, load_sem.at[2]),
        pltpu.make_async_copy(diag_hbm, diag, load_sem.at[0]),
        pltpu.make_async_copy(face_hbm, face, load_sem.at[1]),
        pltpu.make_async_copy(nb_hbm, nb_ref, load_sem.at[3]),
    ]
    for load in loads:
        load.start()

    barrier = pltpu.get_barrier_semaphore()

    def greet(device):
        pl.semaphore_signal(barrier, inc=1, device_id=(device,), device_id_type=MESH)

    def other_plane(d, to):
        return ((z + d) % N_Z) * PLANE + place - core + to

    greet(other_plane(1, 1))
    greet(other_plane(N_Z - 1, 1))

    @pl.when(core == 1)
    def _():
        for d in range(1, PLANE):
            greet(plane0 + (place + d) % PLANE)

        @pl.when(jnp.logical_and(place == PLANE - 1, me < N_DEV - 1))
        def _():
            greet(me + 1)

    @pl.when(core == 0)
    def _():
        greet(me + 1)

        @pl.when(me > 0)
        def _():
            greet(me - 1)

    def tell(reach):
        @pl.when(core == 1)
        def _():
            for d in (reach, N_Z - reach):
                pl.semaphore_signal(
                    ready.at[reach // 2], inc=1, device_id=(other_plane(d, 1),), device_id_type=MESH
                )

    def hear(reach):
        @pl.when(core == 1)
        def _():
            pl.semaphore_wait(ready.at[reach // 2], 2)

    basis[...] = jnp.zeros(basis.shape, F32)
    rows[...] = jnp.zeros(rows.shape, F32)
    loads[0].wait()
    rows[0:ELEM_DEV, 0:WIDTH] = rhs_ref[...]

    def store_row(k, e, tiles):
        for t in range(3):
            lanes = min(128, WIDTH - 128 * t)
            row = jnp.sum(tiles[t], axis=0, keepdims=True)[:, :lanes]
            basis[e, k : k + 1, 128 * t : 128 * t + lanes] = row
            rows[e : e + 1, 128 * t : 128 * t + lanes] = row

    def make_traces():
        got = trace_tiles([rows[:, 128 * t : 128 * t + 128] for t in range(3)])
        for f in range(6):
            traces[f] = got[f]

    for e in range(ELEM_DEV):
        basis[e, 0:1, 0:WIDTH] = rhs_ref[e : e + 1, :]
    make_traces()

    def x_traces(tiles):
        got = trace_tiles(tiles)
        return got[0], got[1]

    def send_x(step, kind):
        for side in range(2):
            @pl.when(me > 0 if side == 0 else me < N_DEV - 1)
            def _():
                x_copy(step, kind, side).start()

    def x_copy(step, kind, side):
        return pltpu.make_async_remote_copy(
            src_ref=out_x.at[step, kind, side],
            dst_ref=in_x[step][kind].at[1 - side],
            send_sem=x_send.at[step, kind, side],
            recv_sem=x_recv.at[step, kind, 1 - side],
            device_id=(me - 1 if side == 0 else me + 1,),
            device_id_type=MESH,
        )

    def wait_x(step, kind):
        for side in range(2):
            @pl.when(me < N_DEV - 1 if side == 0 else me > 0)
            def _():
                x_copy(step, kind, side).wait_recv()

    def far_copy(side):
        return pltpu.make_async_remote_copy(
            src_ref=face.at[:, side],
            dst_ref=far.at[1 - side],
            send_sem=far_send.at[side],
            recv_sem=far_recv.at[1 - side],
            device_id=(me - 1 if side == 0 else me + 1,),
            device_id_type=MESH,
        )

    heard = jnp.where(
        core == 1,
        4 + 15 + 2 - jnp.where(me == N_DEV - 1, 1, 0),
        16 + jnp.where(jnp.logical_and(place == 0, me > 0), 1, 0),
    )
    pl.semaphore_wait(barrier, heard)

    out_x[0, 0, 0] = traces[0]
    out_x[0, 0, 1] = traces[1]
    send_x(0, 0)
    tell(1)
    loads[2].wait()
    for side in range(2):
        @pl.when(me > 0 if side == 0 else me < N_DEV - 1)
        def _():
            far_copy(side).start()
    loads[1].wait()
    loads[3].wait()

    base = me * ELEM_DEV

    def link(e, f):
        wanted = nb_ref[e, f]
        first = base + (-ELEM_DEV if f == 0 else ELEM_DEV if f == 1 else 0)
        return wanted >= 0, jnp.clip(wanted - first, 0, ELEM_DEV - 1)

    links = [[link(e, f) for f in range(6)] for e in range(ELEM_DEV)]

    def own_part(out):
        for e in range(ELEM_DEV):
            total = place_element(matvec(diag[e], rows[e : e + 1, 0:WIDTH]))
            for f in range(2, 6):
                valid, index = links[e][f]
                row = jnp.where(valid, traces[f ^ 1, pl.ds(index, 1), :], 0.0)
                total = add_all(total, place_face(f, matvec(face[e, f], row[:, 0:FACE_WIDTH])))
            out.append(total)

    def x_part(e, across):
        total = None
        for f in range(2):
            part = place_face(f, matvec(face[e, f], across[f][:, 0:FACE_WIDTH]))
            total = part if total is None else add_all(total, part)
        return total

    def received(step, kind, e, f):
        valid, index = links[e][f]
        return valid, in_x[step][kind][f, pl.ds(index, 1), :]

    grams = {}
    for step in range(2):
        k = 2 * step
        own = []
        own_part(own)
        sums = [
            jnp.concatenate([jnp.sum(own[e][t], axis=0, keepdims=True) for e in range(ELEM_DEV)] * 2, axis=0)
            for t in range(3)
        ]
        low, high = x_traces(sums)
        out_x[step, 1, 0] = low
        out_x[step, 1, 1] = high
        send_x(step, 1)
        if step == 0:
            for side in range(2):
                @pl.when(me < N_DEV - 1 if side == 0 else me > 0)
                def _():
                    far_copy(side).wait_recv()
        back = []
        for e in range(ELEM_DEV):
            pair = []
            for f in range(2):
                valid, index = links[e][f]
                trace = traces[f, e : e + 1, 0:FACE_WIDTH]
                pair.append(place_trace(matvec(far[f, index], trace)))
            back.append(pair)
        if step == 1:
            for kk in range(3):
                grams[kk] = gram_column(basis, kk)
        wait_x(step, 0)
        for e in range(ELEM_DEV):
            across = []
            for f in range(2):
                valid, row = received(step, 0, e, f)
                across.append(jnp.where(valid, row, 0.0))
            store_row(k + 1, e, add_all(own[e], x_part(e, across)))
        make_traces()
        own = []
        own_part(own)
        wait_x(step, 1)
        hear(1 + step)
        tell(2 + 2 * step)
        for e in range(ELEM_DEV):
            across = []
            for f in range(2):
                valid, row = received(step, 1, e, f)
                across.append(jnp.where(valid, row + back[e][f], 0.0))
            store_row(k + 2, e, add_all(own[e], x_part(e, across)))
        if step == 0:
            make_traces()
            out_x[1, 0, 0] = traces[0]
            out_x[1, 0, 1] = traces[1]
            send_x(1, 0)

    stores[0].start()
    grams[3] = gram_column(basis, 3)
    grams[4] = gram_column(basis, 4)
    packed = jnp.zeros((8, 128), F32)
    for k in range(BASIS):
        packed = pack(packed, k, grams[k])
    message[0] = packed

    def plane_copy(d):
        return pltpu.make_async_remote_copy(
            src_ref=message.at[0],
            dst_ref=got_plane.at[PLANE - d - 1],
            send_sem=p_send,
            recv_sem=p_recv,
            device_id=(plane0 + (place + d) % PLANE,),
            device_id_type=MESH,
        )

    def z_copy(d, to):
        return pltpu.make_async_remote_copy(
            src_ref=message.at[1],
            dst_ref=got_z.at[(N_Z - d) % N_Z],
            send_sem=z_send,
            recv_sem=z_recv,
            device_id=(other_plane(d, to),),
            device_id_type=MESH,
        )

    def wait_all(ref, sem):
        pltpu.make_async_copy(ref, ref, sem).wait()

    far_first = sorted(range(1, N_Z), key=lambda d: -min(d, N_Z - d))

    @pl.when(core == 1)
    def _():
        for d in range(2, PLANE, 2):
            plane_copy(d).start()
        wait_all(got_plane, p_recv)
        high, low = sum_messages([message[0]] + [got_plane[i] for i in range(PLANE - 1)])
        message[1] = repack(high, low)
        hear(4)
        for d in far_first:
            z_copy(d, 0).start()
        for d in far_first:
            z_copy(d, 1).start()
        z_copy(0, 0).start()
        got_z[0] = message[1]
        wait_all(got_z.at[pl.ds(1, N_Z - 1)], z_recv)

    @pl.when(core == 0)
    def _():
        for d in range(1, PLANE, 2):
            plane_copy(d).start()
        wait_all(got_z, z_recv)

    high, low = sum_messages([got_z[i] for i in range(N_Z)])
    gram[0] = high
    gram[1] = low
    stores[1].start()

    for side in range(2):
        @pl.when(me > 0 if side == 0 else me < N_DEV - 1)
        def _():
            far_copy(side).wait_send()
            for step in range(2):
                for kind in range(2):
                    x_copy(step, kind, side).wait_send()

    @pl.when(core == 1)
    def _():
        wait_all(got_plane.at[pl.ds(0, 15)], p_send)
        wait_all(got_plane.at[pl.ds(0, 2 * N_Z - 1)], z_send)

    @pl.when(core == 0)
    def _():
        wait_all(got_plane.at[pl.ds(0, 16)], p_send)

    for store in stores:
        store.wait()


def finish(basis_hbm, gram_hbm, q_hbm, r_hbm, up_hbm, basis_ref, gram_ref, q_ref, r_ref, up_ref, sem):
    loads = [
        pltpu.make_async_copy(gram_hbm, gram_ref, sem.at[0]),
        pltpu.make_async_copy(basis_hbm, basis_ref, sem.at[1]),
    ]
    stores = [
        pltpu.make_async_copy(q_ref, q_hbm, sem.at[2]),
        pltpu.make_async_copy(r_ref, r_hbm, sem.at[3]),
        pltpu.make_async_copy(up_ref, up_hbm, sem.at[4]),
    ]
    for load in loads:
        load.start()
    loads[0].wait()
    high, low = gram_ref[0], gram_ref[1]
    factors, r, inverse, y = solve(high, low)

    sub, lane = iota((8, 128), 0), iota((8, 128), 1)
    r_tile = jnp.zeros((8, 128), F32)
    for (i, k), value in r.items():
        r_tile = jnp.where(jnp.logical_and(sub == i, lane == k), value, r_tile)
    r_ref[...] = r_tile[0:BASIS, 0:BASIS]
    stores[1].start()
    columns = []
    for j in range(BASIS - 1):
        column = jnp.zeros((8, 128), F32)
        for i in range(j + 1, BASIS):
            column = jnp.where(sub == i, factors[i, j], column)
        columns.append(column)
    scale, weight = jnp.zeros((8, 128), F32), jnp.zeros((8, 128), F32)
    for j in range(BASIS):
        scale = jnp.where(sub == j, inverse[j], scale)
        if j < POWERS:
            weight = jnp.where(sub == j, y[j], weight)
    loads[1].wait()
    for e in range(ELEM_DEV):
        for t in range(3):
            lanes = min(128, WIDTH - 128 * t)
            x = basis_ref[e, :, 128 * t : 128 * t + 128]
            for j in range(BASIS - 1):
                x = x - columns[j] * x[j : j + 1, :]
            x = x * scale
            q_ref[:, e, 128 * t : 128 * t + lanes] = x[0:BASIS, 0:lanes]
            update = jnp.sum(x * weight, axis=0, keepdims=True)
            up_ref[e : e + 1, 128 * t : 128 * t + lanes] = update[:, 0:lanes]
    stores[0].start()
    stores[2].start()
    for store in stores:
        store.wait()


def body(right_side, diag_blocks, face_blocks, neighbours):
    hbm = pl.BlockSpec(memory_space=pl.ANY)
    tile = (8, 128)
    basis, gram = pl.pallas_call(
        kernel,
        out_shape=(
            jax.ShapeDtypeStruct((ELEM_DEV, 8, 384), F32),
            jax.ShapeDtypeStruct((2,) + tile, F32),
        ),
        in_specs=[hbm] * 4,
        out_specs=(hbm, hbm),
        scratch_shapes=[
            pltpu.SMEM((ELEM_DEV, 6), jnp.int32),
            pltpu.VMEM((ELEM_DEV, WIDTH), F32),
            pltpu.VMEM((ELEM_DEV, WIDTH, WIDTH), F32),
            pltpu.VMEM((ELEM_DEV, 6, FACE_WIDTH, FACE_WIDTH), F32),
            pltpu.VMEM((ELEM_DEV, 8, 384), F32),
            pltpu.VMEM((2,) + tile, F32),
            pltpu.VMEM((8, 384), F32),
            pltpu.VMEM((6,) + tile, F32),
            pltpu.VMEM((2, 2, 2) + tile, F32),
            pltpu.VMEM((2,) + tile, F32),
            pltpu.VMEM((2,) + tile, F32),
            pltpu.VMEM((2,) + tile, F32),
            pltpu.VMEM((2,) + tile, F32),
            pltpu.VMEM((2, ELEM_DEV, FACE_WIDTH, FACE_WIDTH), F32),
            pltpu.VMEM((2,) + tile, F32),
            pltpu.VMEM((PLANE - 1,) + tile, F32),
            pltpu.VMEM((N_Z,) + tile, F32),
            pltpu.SemaphoreType.DMA((6,)),
            pltpu.SemaphoreType.DMA((2,)),
            pltpu.SemaphoreType.DMA((2,)),
            pltpu.SemaphoreType.DMA((2, 2, 2)),
            pltpu.SemaphoreType.DMA((2, 2, 2)),
            pltpu.SemaphoreType.DMA,
            pltpu.SemaphoreType.DMA,
            pltpu.SemaphoreType.DMA,
            pltpu.SemaphoreType.DMA,
            pltpu.SemaphoreType.REGULAR((3,)),
        ],
        compiler_params=pltpu.CompilerParams(
            collective_id=0, has_side_effects=True, vmem_limit_bytes=62 * 2**20
        ),
    )(neighbours, right_side, diag_blocks, face_blocks)
    basis_q, r_factor, update = pl.pallas_call(
        finish,
        out_shape=(
            jax.ShapeDtypeStruct((BASIS, ELEM_DEV, WIDTH), F32),
            jax.ShapeDtypeStruct((BASIS, BASIS), F32),
            jax.ShapeDtypeStruct((ELEM_DEV, WIDTH), F32),
        ),
        in_specs=[hbm, hbm],
        out_specs=(hbm, hbm, hbm),
        scratch_shapes=[
            pltpu.VMEM((ELEM_DEV, 8, 384), F32),
            pltpu.VMEM((2,) + tile, F32),
            pltpu.VMEM((BASIS, ELEM_DEV, WIDTH), F32),
            pltpu.VMEM((BASIS, BASIS), F32),
            pltpu.VMEM((ELEM_DEV, WIDTH), F32),
            pltpu.SemaphoreType.DMA((5,)),
        ],
        compiler_params=pltpu.CompilerParams(vmem_limit_bytes=62 * 2**20),
    )(basis, gram)
    return basis_q.transpose(1, 0, 2), r_factor, update


def solution(mesh):
    in_specs = (
        P("elem", None),
        P("elem", None, None),
        P("elem", None, None, None),
        P("elem", None),
    )
    out_specs = (P("elem", None, None), P(), P("elem", None))
    return jax.shard_map(body, mesh=mesh, in_specs=in_specs, out_specs=out_specs, check_vma=False)
```

```python
import jax
import jax.numpy as jnp
from jax import lax
from jax.experimental import pallas as pl
from jax.experimental.pallas import tpu as pltpu
from jax.sharding import PartitionSpec as P

POWERS = 4
BASIS = 5
ELEM_DEV = 4
WIDTH = 320
FACE_WIDTH = 80
N_DEV = 512
PLANE = 32
N_Z = 16
F32 = jnp.float32
MESH = pl.DeviceIdType.MESH


def iota(shape, dim):
    return lax.broadcasted_iota(jnp.int32, shape, dim)


def two_sum(a, b):
    s = a + b
    t = s - a
    return s, (a - (s - t)) + (b - t)


def fast_two_sum(a, b):
    s = a + b
    return s, b - (s - a)


def split(a):
    c = a * 4097.0
    high = c - (c - a)
    return high, a - high


def two_prod(a, b):
    p = a * b
    ah, al = split(a)
    bh, bl = split(b)
    return p, ((ah * bh - p) + ah * bl + al * bh) + al * bl


def trace_tiles(tiles):
    lane = iota((8, 128), 1)
    within, field_odd = lane % 16, (lane // 16) % 2
    u, w = within // 4, within % 4
    offsets = [
        4 * u + w,
        48 + 4 * u + w,
        16 * u + w,
        16 * u + 12 + w,
        16 * u + 4 * w,
        16 * u + 4 * w + 3,
    ]
    out = []
    for offset in offsets:
        index = field_odd * 64 + offset
        got = [jnp.take_along_axis(tile, index, axis=1) for tile in tiles]
        out.append(jnp.where(lane < 32, got[0], jnp.where(lane < 64, got[1], got[2])))
    return out


def face_lane(face, rows, first):
    a = iota((rows, 128), 0) + first
    field_odd, within = (a // 16) % 2, a % 16
    u, w = within // 4, within % 4
    offset = [
        4 * u + w,
        48 + 4 * u + w,
        16 * u + w,
        16 * u + 12 + w,
        16 * u + 4 * w,
        16 * u + 4 * w + 3,
    ][face]
    return field_odd * 64 + offset


def fold(placed):
    return jnp.sum(placed.reshape(-1, 8, 128), axis=0)


def place_element(column):
    out = []
    for tile in range(3):
        rows = min(128, WIDTH - 128 * tile)
        part = jnp.broadcast_to(column[128 * tile : 128 * tile + rows], (rows, 128))
        out.append(fold(jnp.where(iota((rows, 128), 0) == iota((rows, 128), 1), part, 0.0)))
    return out


def place_face(face, column):
    out = []
    for tile in range(3):
        rows = min(32, FACE_WIDTH - 32 * tile)
        part = jnp.broadcast_to(column[32 * tile : 32 * tile + rows], (rows, 128))
        out.append(fold(jnp.where(face_lane(face, rows, 32 * tile) == iota((rows, 128), 1), part, 0.0)))
    return out


def place_trace(column):
    shape = (FACE_WIDTH, 128)
    part = jnp.broadcast_to(column, shape)
    return jnp.sum(jnp.where(iota(shape, 0) == iota(shape, 1), part, 0.0), axis=0, keepdims=True)


def add_all(left, right):
    return [a + b for a, b in zip(left, right)]


def matvec(matrix, row):
    return jnp.sum(matrix * row, axis=1, keepdims=True)


def gram_column(basis, k):
    chains = []
    for tile in range(3):
        total, low = None, None
        for e in range(ELEM_DEV):
            x = basis[e, :, 128 * tile : 128 * tile + 128]
            b = jnp.broadcast_to(basis[e, k : k + 1, 128 * tile : 128 * tile + 128], (8, 128))
            p, err = two_prod(x, b)
            if total is None:
                total, low = p, err
            else:
                total, more = two_sum(total, p)
                low = low + (err + more)
        chains.append((total, low))
    total, low = chains[0]
    for other, other_low in chains[1:]:
        total, more = two_sum(total, other)
        low = low + (other_low + more)
    grid = jnp.minimum(256.0 * jnp.max(jnp.abs(total), axis=1, keepdims=True), 1e38)
    lead = (total + grid) - grid
    rest = (total - lead) + low
    return jnp.sum(lead, axis=1, keepdims=True), jnp.sum(rest, axis=1, keepdims=True)


def pack(message, k, pair):
    lane = iota((8, 128), 1)
    message = jnp.where(lane == k, pair[0], message)
    return jnp.where(lane == 8 + k, pair[1], message)


def sum_messages(tiles):
    chains = []
    for start in range(8):
        mine = tiles[start::8]
        total, low = mine[0], jnp.zeros((8, 128), F32)
        for tile in mine[1:]:
            total, more = two_sum(total, tile)
            low = low + more
        chains.append((total, low))
    while len(chains) > 1:
        merged = []
        for a, b in zip(chains[::2], chains[1::2]):
            total, more = two_sum(a[0], b[0])
            merged.append((total, (a[1] + b[1]) + more))
        chains = merged
    total, low = chains[0]
    return fast_two_sum(total, low + pltpu.roll(total, 120, 1))


def repack(high, low):
    return jnp.where(iota((8, 128), 1) < 8, high, pltpu.roll(low, 8, 1))


def solve(high, low):
    def spread(tile, i, k):
        return jnp.broadcast_to(tile[i : i + 1, k : k + 1], (8, 128))

    g = {(i, k): (spread(high, i, k), spread(low, i, k)) for i in range(BASIS) for k in range(i, BASIS)}
    factors, inverse, r = {}, [], {}
    for j in range(BASIS):
        d, d_low = g[j, j]
        root = lax.rsqrt(d)
        root = root * (1.5 - 0.5 * d * root * root)
        inverse.append(root)
        for k in range(j, BASIS):
            r[j, k] = g[j, k][0] * root
        if j == BASIS - 1:
            break
        recip = 1.0 / d
        ls = {}
        for i in range(j + 1, BASIS):
            t, t_low = g[j, i]
            first = t * recip
            p, err = two_prod(first, d)
            rest = (((t - p) - err) + t_low) - first * d_low
            ls[i] = fast_two_sum(first, rest * recip)
            factors[i, j] = ls[i][0]
        for i in range(j + 1, BASIS):
            for k in range(i, BASIS):
                t, t_low = g[j, k]
                p, err = two_prod(ls[i][0], t)
                err = err + (ls[i][0] * t_low + ls[i][1] * t)
                total, more = two_sum(g[i, k][0], -p)
                g[i, k] = fast_two_sum(total, more + (g[i, k][1] - err))
    h = {}
    for j in range(POWERS):
        for i in range(j + 2):
            value = r[i, j + 1]
            for m in range(max(i - 1, 0), j):
                value = value - h[i, m] * r[m, j]
            h[i, j] = value * inverse[j]
    normal = {}
    for a in range(POWERS):
        for b in range(a, POWERS):
            value = h[0, a] * h[0, b]
            for i in range(1, a + 2):
                value = value + h[i, a] * h[i, b]
            normal[a, b] = value
    target = [r[0, 0] * h[0, a] for a in range(POWERS)]
    lower, recips = {}, []
    for j in range(POWERS):
        recips.append(1.0 / normal[j, j])
        for i in range(j + 1, POWERS):
            lower[i, j] = normal[j, i] * recips[j]
        for i in range(j + 1, POWERS):
            target[i] = target[i] - lower[i, j] * target[j]
            for k in range(i, POWERS):
                normal[i, k] = normal[i, k] - lower[i, j] * normal[j, k]
    y = [target[j] * recips[j] for j in range(POWERS)]
    for j in range(POWERS - 1, -1, -1):
        for i in range(j + 1, POWERS):
            y[j] = y[j] - lower[i, j] * y[i]
    return factors, r, inverse, y


def kernel(
    nb_hbm, rhs_hbm, diag_hbm, face_hbm,
    basis_hbm, gram_hbm,
    nb_ref, rhs_ref, diag, face, basis, gram, rows, traces, out_x, in_a, in_b, in_c, in_d, packed_face, far, message, got_plane, got_z,
    load_sem, far_send, far_recv, x_send, x_recv, p_send, p_recv, z_send, z_recv, ready,
):
    in_x = ((in_a, in_b), (in_c, in_d))
    me = lax.axis_index("elem")
    place, z, core = me % PLANE, me // PLANE, me % 2
    plane0 = me - place

    stores = [
        pltpu.make_async_copy(basis, basis_hbm, load_sem.at[4]),
        pltpu.make_async_copy(gram, gram_hbm, load_sem.at[5]),
    ]
    loads = [
        pltpu.make_async_copy(rhs_hbm, rhs_ref, load_sem.at[2]),
        pltpu.make_async_copy(diag_hbm, diag, load_sem.at[0]),
        pltpu.make_async_copy(face_hbm, face, load_sem.at[1]),
        pltpu.make_async_copy(nb_hbm, nb_ref, load_sem.at[3]),
    ]
    for load in loads:
        load.start()

    barrier = pltpu.get_barrier_semaphore()

    def greet(device):
        pl.semaphore_signal(barrier, inc=1, device_id=(device,), device_id_type=MESH)

    def other_plane(d, to):
        return ((z + d) % N_Z) * PLANE + place - core + to

    @pl.when(core == 1)
    def _():
        greet(plane0 + (place + PLANE - 1) % PLANE)
        greet(plane0 + (place + 1) % PLANE)

        @pl.when(jnp.logical_and(place == PLANE - 1, me < N_DEV - 1))
        def _():
            greet(me + 1)

        for d in range(2, PLANE - 1):
            greet(plane0 + (place + d) % PLANE)

    @pl.when(core == 0)
    def _():
        @pl.when(me > 0)
        def _():
            greet(me - 1)

        greet(me + 1)

    greet(other_plane(1, 1))
    greet(other_plane(N_Z - 1, 1))

    def tell(reach):
        @pl.when(core == 1)
        def _():
            for d in (reach, N_Z - reach):
                pl.semaphore_signal(
                    ready.at[reach // 2], inc=1, device_id=(other_plane(d, 1),), device_id_type=MESH
                )

    def hear(reach):
        @pl.when(core == 1)
        def _():
            pl.semaphore_wait(ready.at[reach // 2], 2)

    basis[...] = jnp.zeros(basis.shape, F32)
    rows[...] = jnp.zeros(rows.shape, F32)
    loads[0].wait()
    rows[0:ELEM_DEV, 0:WIDTH] = rhs_ref[...]

    def store_row(k, e, tiles):
        for t in range(3):
            lanes = min(128, WIDTH - 128 * t)
            row = jnp.sum(tiles[t], axis=0, keepdims=True)[:, :lanes]
            basis[e, k : k + 1, 128 * t : 128 * t + lanes] = row
            rows[e : e + 1, 128 * t : 128 * t + lanes] = row

    def make_traces():
        got = trace_tiles([rows[:, 128 * t : 128 * t + 128] for t in range(3)])
        for f in range(6):
            traces[f] = got[f]

    for e in range(ELEM_DEV):
        basis[e, 0:1, 0:WIDTH] = rhs_ref[e : e + 1, :]
    make_traces()

    def x_traces(tiles):
        got = trace_tiles(tiles)
        return got[0], got[1]

    def send_x(step, kind):
        for side in range(2):
            @pl.when(me > 0 if side == 0 else me < N_DEV - 1)
            def _():
                x_copy(step, kind, side).start()

    def x_copy(step, kind, side):
        return pltpu.make_async_remote_copy(
            src_ref=out_x.at[step, kind, side],
            dst_ref=in_x[step][kind].at[1 - side],
            send_sem=x_send.at[step, kind, side],
            recv_sem=x_recv.at[step, kind, 1 - side],
            device_id=(me - 1 if side == 0 else me + 1,),
            device_id_type=MESH,
        )

    def wait_x(step, kind):
        for side in range(2):
            @pl.when(me < N_DEV - 1 if side == 0 else me > 0)
            def _():
                x_copy(step, kind, side).wait_recv()

    def far_copy(side):
        return pltpu.make_async_remote_copy(
            src_ref=packed_face.at[side],
            dst_ref=far.at[1 - side, pl.ds(0, 3)],
            send_sem=far_send.at[side],
            recv_sem=far_recv.at[1 - side],
            device_id=(me - 1 if side == 0 else me + 1,),
            device_id_type=MESH,
        )

    out_x[0, 0, 0] = traces[0]
    out_x[0, 0, 1] = traces[1]
    loads[2].wait()
    for side in range(2):
        packed_face[side, 2, :, FACE_WIDTH:128] = jnp.zeros((FACE_WIDTH, 48), F32)
        for b in range(3):
            packed_face[side, b, :, 0:FACE_WIDTH] = face[b, side]
        packed_face[side, 0, :, FACE_WIDTH:128] = face[3, side, :, 0:48]
        packed_face[side, 1, :, FACE_WIDTH:128] = jnp.concatenate(
            [face[3, side, :, 48:FACE_WIDTH], jnp.zeros((FACE_WIDTH, 16), F32)], axis=1
        )
    loads[1].wait()
    loads[3].wait()

    base = me * ELEM_DEV

    def link(e, f):
        wanted = nb_ref[e, f]
        first = base + (-ELEM_DEV if f == 0 else ELEM_DEV if f == 1 else 0)
        return wanted >= 0, jnp.clip(wanted - first, 0, ELEM_DEV - 1)

    links = [[link(e, f) for f in range(6)] for e in range(ELEM_DEV)]

    def own_part(out):
        for e in range(ELEM_DEV):
            total = place_element(matvec(diag[e], rows[e : e + 1, 0:WIDTH]))
            for f in range(2, 6):
                valid, index = links[e][f]
                row = jnp.where(valid, traces[f ^ 1, pl.ds(index, 1), :], 0.0)
                total = add_all(total, place_face(f, matvec(face[e, f], row[:, 0:FACE_WIDTH])))
            out.append(total)

    def x_part(e, across):
        total = None
        for f in range(2):
            part = place_face(f, matvec(face[e, f], across[f][:, 0:FACE_WIDTH]))
            total = part if total is None else add_all(total, part)
        return total

    def received(step, kind, e, f):
        valid, index = links[e][f]
        return valid, in_x[step][kind][f, pl.ds(index, 1), :]

    heard = jnp.where(
        core == 1,
        4 + 15 + 2 - jnp.where(me == N_DEV - 1, 1, 0),
        16 + jnp.where(jnp.logical_and(place == 0, me > 0), 1, 0),
    )
    grams = {}
    for step in range(2):
        k = 2 * step
        own = []
        own_part(own)
        sums = [
            jnp.concatenate([jnp.sum(own[e][t], axis=0, keepdims=True) for e in range(ELEM_DEV)] * 2, axis=0)
            for t in range(3)
        ]
        low, high = x_traces(sums)
        out_x[step, 1, 0] = low
        out_x[step, 1, 1] = high
        if step == 0:
            pl.semaphore_wait(barrier, heard)
            send_x(0, 0)
            send_x(0, 1)
            for side in range(2):
                @pl.when(me > 0 if side == 0 else me < N_DEV - 1)
                def _():
                    far_copy(side).start()
            tell(1)
        else:
            send_x(step, 1)
        kept = [[traces[f, e : e + 1, 0:FACE_WIDTH] for f in range(2)] for e in range(ELEM_DEV)]

        def added(e, f):
            return place_trace(matvec(far[f, links[e][f][1], :, 0:FACE_WIDTH], kept[e][f]))

        if step == 1:
            back = [[added(e, f) for f in range(2)] for e in range(ELEM_DEV)]
        if step == 1:
            for kk in range(3):
                grams[kk] = gram_column(basis, kk)
        wait_x(step, 0)
        for e in range(ELEM_DEV):
            across = []
            for f in range(2):
                valid, row = received(step, 0, e, f)
                across.append(jnp.where(valid, row, 0.0))
            store_row(k + 1, e, add_all(own[e], x_part(e, across)))
        make_traces()
        own = []
        own_part(own)
        wait_x(step, 1)
        if step == 0:
            for side in range(2):
                @pl.when(me < N_DEV - 1 if side == 0 else me > 0)
                def _():
                    far_copy(side).wait_recv()
                head = far[1 - side, 0:2, :, FACE_WIDTH:128]
                far[1 - side, 3, :, 0:48] = head[0]
                far[1 - side, 3, :, 48:FACE_WIDTH] = head[1, :, 0:32]
            back = [[added(e, f) for f in range(2)] for e in range(ELEM_DEV)]
        hear(1 + step)
        tell(2 + 2 * step)
        for e in range(ELEM_DEV):
            across = []
            for f in range(2):
                valid, row = received(step, 1, e, f)
                across.append(jnp.where(valid, row + back[e][f], 0.0))
            store_row(k + 2, e, add_all(own[e], x_part(e, across)))
        if step == 0:
            make_traces()
            out_x[1, 0, 0] = traces[0]
            out_x[1, 0, 1] = traces[1]
            send_x(1, 0)

    stores[0].start()
    grams[3] = gram_column(basis, 3)
    grams[4] = gram_column(basis, 4)
    packed = jnp.zeros((8, 128), F32)
    for k in range(BASIS):
        packed = pack(packed, k, grams[k])
    message[0] = packed

    def plane_copy(d):
        return pltpu.make_async_remote_copy(
            src_ref=message.at[0],
            dst_ref=got_plane.at[PLANE - d - 1],
            send_sem=p_send,
            recv_sem=p_recv,
            device_id=(plane0 + (place + d) % PLANE,),
            device_id_type=MESH,
        )

    def z_copy(d, to):
        return pltpu.make_async_remote_copy(
            src_ref=message.at[1],
            dst_ref=got_z.at[(N_Z - d) % N_Z],
            send_sem=z_send,
            recv_sem=z_recv,
            device_id=(other_plane(d, to),),
            device_id_type=MESH,
        )

    def wait_all(ref, sem):
        pltpu.make_async_copy(ref, ref, sem).wait()

    far_first = sorted(range(1, N_Z), key=lambda d: -min(d, N_Z - d))

    @pl.when(core == 1)
    def _():
        for d in range(2, PLANE, 2):
            plane_copy(d).start()
        wait_all(got_plane, p_recv)
        high, low = sum_messages([message[0]] + [got_plane[i] for i in range(PLANE - 1)])
        message[1] = repack(high, low)
        hear(4)
        for d in far_first:
            z_copy(d, 0).start()
            z_copy(d, 1).start()
        z_copy(0, 0).start()
        got_z[0] = message[1]
        wait_all(got_z.at[pl.ds(1, N_Z - 1)], z_recv)

    @pl.when(core == 0)
    def _():
        for d in range(1, PLANE, 2):
            plane_copy(d).start()
        wait_all(got_z, z_recv)

    high, low = sum_messages([got_z[i] for i in range(N_Z)])
    gram[0] = high
    gram[1] = low
    stores[1].start()

    for side in range(2):
        @pl.when(me > 0 if side == 0 else me < N_DEV - 1)
        def _():
            far_copy(side).wait_send()
            for step in range(2):
                for kind in range(2):
                    x_copy(step, kind, side).wait_send()

    @pl.when(core == 1)
    def _():
        wait_all(got_plane.at[pl.ds(0, 15)], p_send)
        wait_all(got_plane.at[pl.ds(0, 2 * N_Z - 1)], z_send)

    @pl.when(core == 0)
    def _():
        wait_all(got_plane.at[pl.ds(0, 16)], p_send)

    for store in stores:
        store.wait()


def finish(basis_hbm, gram_hbm, q_hbm, r_hbm, up_hbm, basis_ref, gram_ref, q_ref, r_ref, up_ref, sem):
    loads = [
        pltpu.make_async_copy(gram_hbm, gram_ref, sem.at[0]),
        pltpu.make_async_copy(basis_hbm, basis_ref, sem.at[1]),
    ]
    stores = [
        pltpu.make_async_copy(q_ref, q_hbm, sem.at[2]),
        pltpu.make_async_copy(r_ref, r_hbm, sem.at[3]),
        pltpu.make_async_copy(up_ref, up_hbm, sem.at[4]),
    ]
    for load in loads:
        load.start()
    loads[0].wait()
    high, low = gram_ref[0], gram_ref[1]
    factors, r, inverse, y = solve(high, low)

    sub, lane = iota((8, 128), 0), iota((8, 128), 1)
    r_tile = jnp.zeros((8, 128), F32)
    for (i, k), value in r.items():
        r_tile = jnp.where(jnp.logical_and(sub == i, lane == k), value, r_tile)
    r_ref[...] = r_tile[0:BASIS, 0:BASIS]
    stores[1].start()
    columns = []
    for j in range(BASIS - 1):
        column = jnp.zeros((8, 128), F32)
        for i in range(j + 1, BASIS):
            column = jnp.where(sub == i, factors[i, j], column)
        columns.append(column)
    scale, weight = jnp.zeros((8, 128), F32), jnp.zeros((8, 128), F32)
    for j in range(BASIS):
        scale = jnp.where(sub == j, inverse[j], scale)
        if j < POWERS:
            weight = jnp.where(sub == j, y[j], weight)
    loads[1].wait()
    for e in range(ELEM_DEV):
        for t in range(3):
            lanes = min(128, WIDTH - 128 * t)
            x = basis_ref[e, :, 128 * t : 128 * t + 128]
            for j in range(BASIS - 1):
                x = x - columns[j] * x[j : j + 1, :]
            x = x * scale
            q_ref[:, e, 128 * t : 128 * t + lanes] = x[0:BASIS, 0:lanes]
            update = jnp.sum(x * weight, axis=0, keepdims=True)
            up_ref[e : e + 1, 128 * t : 128 * t + lanes] = update[:, 0:lanes]
    stores[0].start()
    stores[2].start()
    for store in stores:
        store.wait()


def body(right_side, diag_blocks, face_blocks, neighbours):
    hbm = pl.BlockSpec(memory_space=pl.ANY)
    tile = (8, 128)
    basis, gram = pl.pallas_call(
        kernel,
        out_shape=(
            jax.ShapeDtypeStruct((ELEM_DEV, 8, 384), F32),
            jax.ShapeDtypeStruct((2,) + tile, F32),
        ),
        in_specs=[hbm] * 4,
        out_specs=(hbm, hbm),
        scratch_shapes=[
            pltpu.SMEM((ELEM_DEV, 6), jnp.int32),
            pltpu.VMEM((ELEM_DEV, WIDTH), F32),
            pltpu.VMEM((ELEM_DEV, WIDTH, WIDTH), F32),
            pltpu.VMEM((ELEM_DEV, 6, FACE_WIDTH, FACE_WIDTH), F32),
            pltpu.VMEM((ELEM_DEV, 8, 384), F32),
            pltpu.VMEM((2,) + tile, F32),
            pltpu.VMEM((8, 384), F32),
            pltpu.VMEM((6,) + tile, F32),
            pltpu.VMEM((2, 2, 2) + tile, F32),
            pltpu.VMEM((2,) + tile, F32),
            pltpu.VMEM((2,) + tile, F32),
            pltpu.VMEM((2,) + tile, F32),
            pltpu.VMEM((2,) + tile, F32),
            pltpu.VMEM((2, 3, FACE_WIDTH, 128), F32),
            pltpu.VMEM((2, ELEM_DEV, FACE_WIDTH, 128), F32),
            pltpu.VMEM((2,) + tile, F32),
            pltpu.VMEM((PLANE - 1,) + tile, F32),
            pltpu.VMEM((N_Z,) + tile, F32),
            pltpu.SemaphoreType.DMA((6,)),
            pltpu.SemaphoreType.DMA((2,)),
            pltpu.SemaphoreType.DMA((2,)),
            pltpu.SemaphoreType.DMA((2, 2, 2)),
            pltpu.SemaphoreType.DMA((2, 2, 2)),
            pltpu.SemaphoreType.DMA,
            pltpu.SemaphoreType.DMA,
            pltpu.SemaphoreType.DMA,
            pltpu.SemaphoreType.DMA,
            pltpu.SemaphoreType.REGULAR((3,)),
        ],
        compiler_params=pltpu.CompilerParams(
            collective_id=0, has_side_effects=True, vmem_limit_bytes=62 * 2**20
        ),
    )(neighbours, right_side, diag_blocks, face_blocks)
    basis_q, r_factor, update = pl.pallas_call(
        finish,
        out_shape=(
            jax.ShapeDtypeStruct((BASIS, ELEM_DEV, WIDTH), F32),
            jax.ShapeDtypeStruct((BASIS, BASIS), F32),
            jax.ShapeDtypeStruct((ELEM_DEV, WIDTH), F32),
        ),
        in_specs=[hbm, hbm],
        out_specs=(hbm, hbm, hbm),
        scratch_shapes=[
            pltpu.VMEM((ELEM_DEV, 8, 384), F32),
            pltpu.VMEM((2,) + tile, F32),
            pltpu.VMEM((BASIS, ELEM_DEV, WIDTH), F32),
            pltpu.VMEM((BASIS, BASIS), F32),
            pltpu.VMEM((ELEM_DEV, WIDTH), F32),
            pltpu.SemaphoreType.DMA((5,)),
        ],
        compiler_params=pltpu.CompilerParams(vmem_limit_bytes=62 * 2**20),
    )(basis, gram)
    return basis_q.transpose(1, 0, 2), r_factor, update


def solution(mesh):
    in_specs = (
        P("elem", None),
        P("elem", None, None),
        P("elem", None, None, None),
        P("elem", None),
    )
    out_specs = (P("elem", None, None), P(), P("elem", None))
    return jax.shard_map(body, mesh=mesh, in_specs=in_specs, out_specs=out_specs, check_vma=False)
```

```python
import jax
import jax.numpy as jnp
from jax import lax
from jax.experimental import pallas as pl
from jax.experimental.pallas import tpu as pltpu
from jax.sharding import PartitionSpec as P

POWERS = 4
BASIS = 5
ELEM_DEV = 4
WIDTH = 320
FACE_WIDTH = 80
N_DEV = 512
PLANE = 32
N_Z = 16
F32 = jnp.float32
MESH = pl.DeviceIdType.MESH


def iota(shape, dim):
    return lax.broadcasted_iota(jnp.int32, shape, dim)


def two_sum(a, b):
    s = a + b
    t = s - a
    return s, (a - (s - t)) + (b - t)


def fast_two_sum(a, b):
    s = a + b
    return s, b - (s - a)


def split(a):
    c = a * 4097.0
    high = c - (c - a)
    return high, a - high


def two_prod(a, b):
    p = a * b
    ah, al = split(a)
    bh, bl = split(b)
    return p, ((ah * bh - p) + ah * bl + al * bh) + al * bl


def trace_tiles(tiles):
    lane = iota((8, 128), 1)
    within, field_odd = lane % 16, (lane // 16) % 2
    u, w = within // 4, within % 4
    offsets = [
        4 * u + w,
        48 + 4 * u + w,
        16 * u + w,
        16 * u + 12 + w,
        16 * u + 4 * w,
        16 * u + 4 * w + 3,
    ]
    out = []
    for offset in offsets:
        index = field_odd * 64 + offset
        got = [jnp.take_along_axis(tile, index, axis=1) for tile in tiles]
        out.append(jnp.where(lane < 32, got[0], jnp.where(lane < 64, got[1], got[2])))
    return out


def face_lane(face, rows, first):
    a = iota((rows, 128), 0) + first
    field_odd, within = (a // 16) % 2, a % 16
    u, w = within // 4, within % 4
    offset = [
        4 * u + w,
        48 + 4 * u + w,
        16 * u + w,
        16 * u + 12 + w,
        16 * u + 4 * w,
        16 * u + 4 * w + 3,
    ][face]
    return field_odd * 64 + offset


def fold(placed):
    return jnp.sum(placed.reshape(-1, 8, 128), axis=0)


def place_element(column):
    out = []
    for tile in range(3):
        rows = min(128, WIDTH - 128 * tile)
        part = jnp.broadcast_to(column[128 * tile : 128 * tile + rows], (rows, 128))
        out.append(fold(jnp.where(iota((rows, 128), 0) == iota((rows, 128), 1), part, 0.0)))
    return out


def place_face(face, column):
    out = []
    for tile in range(3):
        rows = min(32, FACE_WIDTH - 32 * tile)
        part = jnp.broadcast_to(column[32 * tile : 32 * tile + rows], (rows, 128))
        out.append(fold(jnp.where(face_lane(face, rows, 32 * tile) == iota((rows, 128), 1), part, 0.0)))
    return out


def place_trace(column):
    shape = (FACE_WIDTH, 128)
    part = jnp.broadcast_to(column, shape)
    return jnp.sum(jnp.where(iota(shape, 0) == iota(shape, 1), part, 0.0), axis=0, keepdims=True)


def add_all(left, right):
    return [a + b for a, b in zip(left, right)]


def matvec(matrix, row):
    return jnp.sum(matrix * row, axis=1, keepdims=True)


def gram_column(basis, k):
    chains = []
    for tile in range(3):
        total, low = None, None
        for e in range(ELEM_DEV):
            x = basis[e, :, 128 * tile : 128 * tile + 128]
            b = jnp.broadcast_to(basis[e, k : k + 1, 128 * tile : 128 * tile + 128], (8, 128))
            p, err = two_prod(x, b)
            if total is None:
                total, low = p, err
            else:
                total, more = two_sum(total, p)
                low = low + (err + more)
        chains.append((total, low))
    total, low = chains[0]
    for other, other_low in chains[1:]:
        total, more = two_sum(total, other)
        low = low + (other_low + more)
    grid = jnp.minimum(256.0 * jnp.max(jnp.abs(total), axis=1, keepdims=True), 1e38)
    lead = (total + grid) - grid
    rest = (total - lead) + low
    return jnp.sum(lead, axis=1, keepdims=True), jnp.sum(rest, axis=1, keepdims=True)


def pack(message, k, pair):
    lane = iota((8, 128), 1)
    message = jnp.where(lane == k, pair[0], message)
    return jnp.where(lane == 8 + k, pair[1], message)


def sum_messages(tiles):
    chains = []
    for start in range(8):
        mine = tiles[start::8]
        total, low = mine[0], jnp.zeros((8, 128), F32)
        for tile in mine[1:]:
            total, more = two_sum(total, tile)
            low = low + more
        chains.append((total, low))
    while len(chains) > 1:
        merged = []
        for a, b in zip(chains[::2], chains[1::2]):
            total, more = two_sum(a[0], b[0])
            merged.append((total, (a[1] + b[1]) + more))
        chains = merged
    total, low = chains[0]
    return fast_two_sum(total, low + pltpu.roll(total, 120, 1))


def repack(high, low):
    return jnp.where(iota((8, 128), 1) < 8, high, pltpu.roll(low, 8, 1))


def solve(high, low):
    def spread(tile, i, k):
        return jnp.broadcast_to(tile[i : i + 1, k : k + 1], (8, 128))

    g = {(i, k): (spread(high, i, k), spread(low, i, k)) for i in range(BASIS) for k in range(i, BASIS)}
    factors, inverse, r = {}, [], {}
    for j in range(BASIS):
        d, d_low = g[j, j]
        root = lax.rsqrt(d)
        root = root * (1.5 - 0.5 * d * root * root)
        inverse.append(root)
        for k in range(j, BASIS):
            r[j, k] = g[j, k][0] * root
        if j == BASIS - 1:
            break
        recip = 1.0 / d
        ls = {}
        for i in range(j + 1, BASIS):
            t, t_low = g[j, i]
            first = t * recip
            p, err = two_prod(first, d)
            rest = (((t - p) - err) + t_low) - first * d_low
            ls[i] = fast_two_sum(first, rest * recip)
            factors[i, j] = ls[i][0]
        for i in range(j + 1, BASIS):
            for k in range(i, BASIS):
                t, t_low = g[j, k]
                p, err = two_prod(ls[i][0], t)
                err = err + (ls[i][0] * t_low + ls[i][1] * t)
                total, more = two_sum(g[i, k][0], -p)
                g[i, k] = fast_two_sum(total, more + (g[i, k][1] - err))
    h = {}
    for j in range(POWERS):
        for i in range(j + 2):
            value = r[i, j + 1]
            for m in range(max(i - 1, 0), j):
                value = value - h[i, m] * r[m, j]
            h[i, j] = value * inverse[j]
    normal = {}
    for a in range(POWERS):
        for b in range(a, POWERS):
            value = h[0, a] * h[0, b]
            for i in range(1, a + 2):
                value = value + h[i, a] * h[i, b]
            normal[a, b] = value
    target = [r[0, 0] * h[0, a] for a in range(POWERS)]
    lower, recips = {}, []
    for j in range(POWERS):
        recips.append(1.0 / normal[j, j])
        for i in range(j + 1, POWERS):
            lower[i, j] = normal[j, i] * recips[j]
        for i in range(j + 1, POWERS):
            target[i] = target[i] - lower[i, j] * target[j]
            for k in range(i, POWERS):
                normal[i, k] = normal[i, k] - lower[i, j] * normal[j, k]
    y = [target[j] * recips[j] for j in range(POWERS)]
    for j in range(POWERS - 1, -1, -1):
        for i in range(j + 1, POWERS):
            y[j] = y[j] - lower[i, j] * y[i]
    return factors, r, inverse, y


def kernel(
    nb_hbm, rhs_hbm, diag_hbm, face_hbm,
    basis, gram,
    nb_ref, rhs_ref, diag, face, rows, traces, out_x, in_a, in_b, in_c, in_d, packed_face, far, message, got_plane, got_z,
    load_sem, far_send, far_recv, x_send, x_recv, p_send, p_recv, z_send, z_recv, ready,
):
    in_x = ((in_a, in_b), (in_c, in_d))
    me = lax.axis_index("elem")
    place, z, core = me % PLANE, me // PLANE, me % 2
    plane0 = me - place

    loads = [
        pltpu.make_async_copy(rhs_hbm, rhs_ref, load_sem.at[2]),
        pltpu.make_async_copy(diag_hbm, diag, load_sem.at[0]),
        pltpu.make_async_copy(face_hbm, face, load_sem.at[1]),
        pltpu.make_async_copy(nb_hbm, nb_ref, load_sem.at[3]),
    ]
    for load in loads:
        load.start()

    barrier = pltpu.get_barrier_semaphore()

    def greet(device):
        pl.semaphore_signal(barrier, inc=1, device_id=(device,), device_id_type=MESH)

    def other_plane(d, to):
        return ((z + d) % N_Z) * PLANE + place - core + to

    @pl.when(core == 1)
    def _():
        greet(plane0 + (place + PLANE - 1) % PLANE)
        greet(plane0 + (place + 1) % PLANE)

        @pl.when(jnp.logical_and(place == PLANE - 1, me < N_DEV - 1))
        def _():
            greet(me + 1)

        for d in range(2, PLANE - 1):
            greet(plane0 + (place + d) % PLANE)

    @pl.when(core == 0)
    def _():
        @pl.when(me > 0)
        def _():
            greet(me - 1)

        greet(me + 1)

    greet(other_plane(1, 1))
    greet(other_plane(N_Z - 1, 1))

    def tell(reach):
        @pl.when(core == 1)
        def _():
            for d in (reach, N_Z - reach):
                pl.semaphore_signal(
                    ready.at[reach // 2], inc=1, device_id=(other_plane(d, 1),), device_id_type=MESH
                )

    def hear(reach):
        @pl.when(core == 1)
        def _():
            pl.semaphore_wait(ready.at[reach // 2], 2)

    basis[...] = jnp.zeros(basis.shape, F32)
    rows[...] = jnp.zeros(rows.shape, F32)
    loads[0].wait()
    rows[0:ELEM_DEV, 0:WIDTH] = rhs_ref[...]

    def store_row(k, e, tiles):
        for t in range(3):
            lanes = min(128, WIDTH - 128 * t)
            row = jnp.sum(tiles[t], axis=0, keepdims=True)[:, :lanes]
            basis[e, k : k + 1, 128 * t : 128 * t + lanes] = row
            rows[e : e + 1, 128 * t : 128 * t + lanes] = row

    def make_traces():
        got = trace_tiles([rows[:, 128 * t : 128 * t + 128] for t in range(3)])
        for f in range(6):
            traces[f] = got[f]

    for e in range(ELEM_DEV):
        basis[e, 0:1, 0:WIDTH] = rhs_ref[e : e + 1, :]
    make_traces()

    def x_traces(tiles):
        got = trace_tiles(tiles)
        return got[0], got[1]

    def send_x(step, kind):
        for side in range(2):
            @pl.when(me > 0 if side == 0 else me < N_DEV - 1)
            def _():
                x_copy(step, kind, side).start()

    def x_copy(step, kind, side):
        return pltpu.make_async_remote_copy(
            src_ref=out_x.at[step, kind, side],
            dst_ref=in_x[step][kind].at[1 - side],
            send_sem=x_send.at[step, kind, side],
            recv_sem=x_recv.at[step, kind, 1 - side],
            device_id=(me - 1 if side == 0 else me + 1,),
            device_id_type=MESH,
        )

    def wait_x(step, kind):
        for side in range(2):
            @pl.when(me < N_DEV - 1 if side == 0 else me > 0)
            def _():
                x_copy(step, kind, side).wait_recv()

    def far_copy(side):
        return pltpu.make_async_remote_copy(
            src_ref=packed_face.at[side],
            dst_ref=far.at[1 - side, pl.ds(0, 3)],
            send_sem=far_send.at[side],
            recv_sem=far_recv.at[1 - side],
            device_id=(me - 1 if side == 0 else me + 1,),
            device_id_type=MESH,
        )

    out_x[0, 0, 0] = traces[0]
    out_x[0, 0, 1] = traces[1]
    loads[2].wait()
    for side in range(2):
        packed_face[side, 2, :, FACE_WIDTH:128] = jnp.zeros((FACE_WIDTH, 48), F32)
        for b in range(3):
            packed_face[side, b, :, 0:FACE_WIDTH] = face[b, side]
        packed_face[side, 0, :, FACE_WIDTH:128] = face[3, side, :, 0:48]
        packed_face[side, 1, :, FACE_WIDTH:128] = jnp.concatenate(
            [face[3, side, :, 48:FACE_WIDTH], jnp.zeros((FACE_WIDTH, 16), F32)], axis=1
        )
    loads[1].wait()
    loads[3].wait()

    base = me * ELEM_DEV

    def link(e, f):
        wanted = nb_ref[e, f]
        first = base + (-ELEM_DEV if f == 0 else ELEM_DEV if f == 1 else 0)
        return wanted >= 0, jnp.clip(wanted - first, 0, ELEM_DEV - 1)

    links = [[link(e, f) for f in range(6)] for e in range(ELEM_DEV)]

    def own_part(out):
        for e in range(ELEM_DEV):
            total = place_element(matvec(diag[e], rows[e : e + 1, 0:WIDTH]))
            for f in range(2, 6):
                valid, index = links[e][f]
                row = jnp.where(valid, traces[f ^ 1, pl.ds(index, 1), :], 0.0)
                total = add_all(total, place_face(f, matvec(face[e, f], row[:, 0:FACE_WIDTH])))
            out.append(total)

    def x_part(e, across):
        total = None
        for f in range(2):
            part = place_face(f, matvec(face[e, f], across[f][:, 0:FACE_WIDTH]))
            total = part if total is None else add_all(total, part)
        return total

    def received(step, kind, e, f):
        valid, index = links[e][f]
        return valid, in_x[step][kind][f, pl.ds(index, 1), :]

    heard = jnp.where(
        core == 1,
        4 + 15 + 2 - jnp.where(me == N_DEV - 1, 1, 0),
        16 + jnp.where(jnp.logical_and(place == 0, me > 0), 1, 0),
    )
    grams = {}
    for step in range(2):
        k = 2 * step
        own = []
        own_part(own)
        sums = [
            jnp.concatenate([jnp.sum(own[e][t], axis=0, keepdims=True) for e in range(ELEM_DEV)] * 2, axis=0)
            for t in range(3)
        ]
        low, high = x_traces(sums)
        out_x[step, 1, 0] = low
        out_x[step, 1, 1] = high
        if step == 0:
            pl.semaphore_wait(barrier, heard)
            send_x(0, 0)
            send_x(0, 1)
            for side in range(2):
                @pl.when(me > 0 if side == 0 else me < N_DEV - 1)
                def _():
                    far_copy(side).start()
            tell(1)
        else:
            send_x(step, 1)
        kept = [[traces[f, e : e + 1, 0:FACE_WIDTH] for f in range(2)] for e in range(ELEM_DEV)]

        def added(e, f):
            return place_trace(matvec(far[f, links[e][f][1], :, 0:FACE_WIDTH], kept[e][f]))

        if step == 1:
            back = [[added(e, f) for f in range(2)] for e in range(ELEM_DEV)]
        if step == 1:
            for kk in range(3):
                grams[kk] = gram_column(basis, kk)
        wait_x(step, 0)
        for e in range(ELEM_DEV):
            across = []
            for f in range(2):
                valid, row = received(step, 0, e, f)
                across.append(jnp.where(valid, row, 0.0))
            store_row(k + 1, e, add_all(own[e], x_part(e, across)))
        make_traces()
        own = []
        own_part(own)
        wait_x(step, 1)
        if step == 0:
            for side in range(2):
                @pl.when(me < N_DEV - 1 if side == 0 else me > 0)
                def _():
                    far_copy(side).wait_recv()
                head = far[1 - side, 0:2, :, FACE_WIDTH:128]
                far[1 - side, 3, :, 0:48] = head[0]
                far[1 - side, 3, :, 48:FACE_WIDTH] = head[1, :, 0:32]
            back = [[added(e, f) for f in range(2)] for e in range(ELEM_DEV)]
        hear(1 + step)
        tell(2 + 2 * step)
        for e in range(ELEM_DEV):
            across = []
            for f in range(2):
                valid, row = received(step, 1, e, f)
                across.append(jnp.where(valid, row + back[e][f], 0.0))
            store_row(k + 2, e, add_all(own[e], x_part(e, across)))
        if step == 0:
            make_traces()
            out_x[1, 0, 0] = traces[0]
            out_x[1, 0, 1] = traces[1]
            send_x(1, 0)

    grams[3] = gram_column(basis, 3)
    grams[4] = gram_column(basis, 4)
    packed = jnp.zeros((8, 128), F32)
    for k in range(BASIS):
        packed = pack(packed, k, grams[k])
    message[0] = packed

    def plane_copy(d):
        return pltpu.make_async_remote_copy(
            src_ref=message.at[0],
            dst_ref=got_plane.at[PLANE - d - 1],
            send_sem=p_send,
            recv_sem=p_recv,
            device_id=(plane0 + (place + d) % PLANE,),
            device_id_type=MESH,
        )

    def z_copy(d, to):
        return pltpu.make_async_remote_copy(
            src_ref=message.at[1],
            dst_ref=got_z.at[(N_Z - d) % N_Z],
            send_sem=z_send,
            recv_sem=z_recv,
            device_id=(other_plane(d, to),),
            device_id_type=MESH,
        )

    def wait_all(ref, sem):
        pltpu.make_async_copy(ref, ref, sem).wait()

    far_first = sorted(range(1, N_Z), key=lambda d: -min(d, N_Z - d))

    @pl.when(core == 1)
    def _():
        for d in range(2, PLANE, 2):
            plane_copy(d).start()
        wait_all(got_plane, p_recv)
        high, low = sum_messages([message[0]] + [got_plane[i] for i in range(PLANE - 1)])
        message[1] = repack(high, low)
        hear(4)
        for d in far_first:
            z_copy(d, 0).start()
            z_copy(d, 1).start()
        z_copy(0, 0).start()
        got_z[0] = message[1]
        wait_all(got_z.at[pl.ds(1, N_Z - 1)], z_recv)

    @pl.when(core == 0)
    def _():
        for d in range(1, PLANE, 2):
            plane_copy(d).start()
        wait_all(got_z, z_recv)

    high, low = sum_messages([got_z[i] for i in range(N_Z)])
    gram[0] = high
    gram[1] = low

    for side in range(2):
        @pl.when(me > 0 if side == 0 else me < N_DEV - 1)
        def _():
            far_copy(side).wait_send()
            for step in range(2):
                for kind in range(2):
                    x_copy(step, kind, side).wait_send()

    @pl.when(core == 1)
    def _():
        wait_all(got_plane.at[pl.ds(0, 15)], p_send)
        wait_all(got_plane.at[pl.ds(0, 2 * N_Z - 1)], z_send)

    @pl.when(core == 0)
    def _():
        wait_all(got_plane.at[pl.ds(0, 16)], p_send)


def finish(basis_ref, gram_ref, q_hbm, r_hbm, up_hbm, q_ref, r_ref, up_ref, sem):
    stores = [
        pltpu.make_async_copy(q_ref, q_hbm, sem.at[0]),
        pltpu.make_async_copy(r_ref, r_hbm, sem.at[1]),
        pltpu.make_async_copy(up_ref, up_hbm, sem.at[2]),
    ]
    high, low = gram_ref[0], gram_ref[1]
    factors, r, inverse, y = solve(high, low)

    sub, lane = iota((8, 128), 0), iota((8, 128), 1)
    r_tile = jnp.zeros((8, 128), F32)
    for (i, k), value in r.items():
        r_tile = jnp.where(jnp.logical_and(sub == i, lane == k), value, r_tile)
    r_ref[...] = r_tile[0:BASIS, 0:BASIS]
    stores[1].start()
    columns = []
    for j in range(BASIS - 1):
        column = jnp.zeros((8, 128), F32)
        for i in range(j + 1, BASIS):
            column = jnp.where(sub == i, factors[i, j], column)
        columns.append(column)
    scale, weight = jnp.zeros((8, 128), F32), jnp.zeros((8, 128), F32)
    for j in range(BASIS):
        scale = jnp.where(sub == j, inverse[j], scale)
        if j < POWERS:
            weight = jnp.where(sub == j, y[j], weight)
    for e in range(ELEM_DEV):
        for t in range(3):
            lanes = min(128, WIDTH - 128 * t)
            x = basis_ref[e, :, 128 * t : 128 * t + 128]
            for j in range(BASIS - 1):
                x = x - columns[j] * x[j : j + 1, :]
            x = x * scale
            q_ref[:, e, 128 * t : 128 * t + lanes] = x[0:BASIS, 0:lanes]
            update = jnp.sum(x * weight, axis=0, keepdims=True)
            up_ref[e : e + 1, 128 * t : 128 * t + lanes] = update[:, 0:lanes]
    stores[0].start()
    stores[2].start()
    for store in stores:
        store.wait()


def body(right_side, diag_blocks, face_blocks, neighbours):
    hbm = pl.BlockSpec(memory_space=pl.ANY)
    vmem = pl.BlockSpec(memory_space=pltpu.VMEM)
    tile = (8, 128)
    operands = [
        pltpu.with_memory_space_constraint(x, pltpu.HBM)
        for x in (neighbours, right_side, diag_blocks, face_blocks)
    ]
    basis, gram = pl.pallas_call(
        kernel,
        out_shape=(
            pltpu.VMEM((ELEM_DEV, 8, 384), F32),
            pltpu.VMEM((2,) + tile, F32),
        ),
        in_specs=[hbm] * 4,
        out_specs=(vmem, vmem),
        scratch_shapes=[
            pltpu.SMEM((ELEM_DEV, 6), jnp.int32),
            pltpu.VMEM((ELEM_DEV, WIDTH), F32),
            pltpu.VMEM((ELEM_DEV, WIDTH, WIDTH), F32),
            pltpu.VMEM((ELEM_DEV, 6, FACE_WIDTH, FACE_WIDTH), F32),
            pltpu.VMEM((8, 384), F32),
            pltpu.VMEM((6,) + tile, F32),
            pltpu.VMEM((2, 2, 2) + tile, F32),
            pltpu.VMEM((2,) + tile, F32),
            pltpu.VMEM((2,) + tile, F32),
            pltpu.VMEM((2,) + tile, F32),
            pltpu.VMEM((2,) + tile, F32),
            pltpu.VMEM((2, 3, FACE_WIDTH, 128), F32),
            pltpu.VMEM((2, ELEM_DEV, FACE_WIDTH, 128), F32),
            pltpu.VMEM((2,) + tile, F32),
            pltpu.VMEM((PLANE - 1,) + tile, F32),
            pltpu.VMEM((N_Z,) + tile, F32),
            pltpu.SemaphoreType.DMA((4,)),
            pltpu.SemaphoreType.DMA((2,)),
            pltpu.SemaphoreType.DMA((2,)),
            pltpu.SemaphoreType.DMA((2, 2, 2)),
            pltpu.SemaphoreType.DMA((2, 2, 2)),
            pltpu.SemaphoreType.DMA,
            pltpu.SemaphoreType.DMA,
            pltpu.SemaphoreType.DMA,
            pltpu.SemaphoreType.DMA,
            pltpu.SemaphoreType.REGULAR((3,)),
        ],
        compiler_params=pltpu.CompilerParams(
            collective_id=0, has_side_effects=True, vmem_limit_bytes=24 * 2**20
        ),
    )(*operands)
    basis_q, r_factor, update = pl.pallas_call(
        finish,
        out_shape=(
            jax.ShapeDtypeStruct((BASIS, ELEM_DEV, WIDTH), F32),
            jax.ShapeDtypeStruct((BASIS, BASIS), F32),
            jax.ShapeDtypeStruct((ELEM_DEV, WIDTH), F32),
        ),
        in_specs=[vmem, vmem],
        out_specs=(hbm, hbm, hbm),
        scratch_shapes=[
            pltpu.VMEM((BASIS, ELEM_DEV, WIDTH), F32),
            pltpu.VMEM((BASIS, BASIS), F32),
            pltpu.VMEM((ELEM_DEV, WIDTH), F32),
            pltpu.SemaphoreType.DMA((3,)),
        ],
        compiler_params=pltpu.CompilerParams(vmem_limit_bytes=4 * 2**20),
    )(basis, gram)
    return basis_q.transpose(1, 0, 2), r_factor, update


def solution(mesh):
    in_specs = (
        P("elem", None),
        P("elem", None, None),
        P("elem", None, None, None),
        P("elem", None),
    )
    out_specs = (P("elem", None, None), P(), P("elem", None))
    return jax.shard_map(body, mesh=mesh, in_specs=in_specs, out_specs=out_specs, check_vma=False)
```

```python
import jax
import jax.numpy as jnp
from jax import lax
from jax.experimental import pallas as pl
from jax.experimental.pallas import tpu as pltpu
from jax.sharding import PartitionSpec as P

POWERS = 4
BASIS = 5
ELEM_DEV = 4
WIDTH = 320
FACE_WIDTH = 80
N_DEV = 512
PLANE = 32
N_Z = 16
F32 = jnp.float32
MESH = pl.DeviceIdType.MESH


def iota(shape, dim):
    return lax.broadcasted_iota(jnp.int32, shape, dim)


def two_sum(a, b):
    s = a + b
    t = s - a
    return s, (a - (s - t)) + (b - t)


def fast_two_sum(a, b):
    s = a + b
    return s, b - (s - a)


def split(a):
    c = a * 4097.0
    high = c - (c - a)
    return high, a - high


def two_prod(a, b):
    p = a * b
    ah, al = split(a)
    bh, bl = split(b)
    return p, ((ah * bh - p) + ah * bl + al * bh) + al * bl


def trace_tiles(tiles):
    lane = iota((8, 128), 1)
    within, field_odd = lane % 16, (lane // 16) % 2
    u, w = within // 4, within % 4
    offsets = [
        4 * u + w,
        48 + 4 * u + w,
        16 * u + w,
        16 * u + 12 + w,
        16 * u + 4 * w,
        16 * u + 4 * w + 3,
    ]
    out = []
    for offset in offsets:
        index = field_odd * 64 + offset
        got = [jnp.take_along_axis(tile, index, axis=1) for tile in tiles]
        out.append(jnp.where(lane < 32, got[0], jnp.where(lane < 64, got[1], got[2])))
    return out


def face_lane(face, rows, first):
    a = iota((rows, 128), 0) + first
    field_odd, within = (a // 16) % 2, a % 16
    u, w = within // 4, within % 4
    offset = [
        4 * u + w,
        48 + 4 * u + w,
        16 * u + w,
        16 * u + 12 + w,
        16 * u + 4 * w,
        16 * u + 4 * w + 3,
    ][face]
    return field_odd * 64 + offset


def fold(placed):
    return jnp.sum(placed.reshape(-1, 8, 128), axis=0)


def place_element(column):
    out = []
    for tile in range(3):
        rows = min(128, WIDTH - 128 * tile)
        part = jnp.broadcast_to(column[128 * tile : 128 * tile + rows], (rows, 128))
        out.append(fold(jnp.where(iota((rows, 128), 0) == iota((rows, 128), 1), part, 0.0)))
    return out


def place_face(face, column):
    out = []
    for tile in range(3):
        rows = min(32, FACE_WIDTH - 32 * tile)
        part = jnp.broadcast_to(column[32 * tile : 32 * tile + rows], (rows, 128))
        out.append(fold(jnp.where(face_lane(face, rows, 32 * tile) == iota((rows, 128), 1), part, 0.0)))
    return out


def place_trace(column):
    shape = (FACE_WIDTH, 128)
    part = jnp.broadcast_to(column, shape)
    return jnp.sum(jnp.where(iota(shape, 0) == iota(shape, 1), part, 0.0), axis=0, keepdims=True)


def add_all(left, right):
    return [a + b for a, b in zip(left, right)]


def matvec(matrix, row):
    return jnp.sum(matrix * row, axis=1, keepdims=True)


def own_column(diag, face_y, face_z, row, across):
    part = diag[:, 0:128] * row[:, 0:128] + diag[:, 128:256] * row[:, 128:256]
    last = diag[:, 256:WIDTH] * row[:, 256:WIDTH]
    part = part + jnp.concatenate([last, jnp.zeros((WIDTH, 384 - WIDTH), F32)], axis=1)
    sub = iota((8, 128), 0) % 4
    both_z = jnp.where(sub == 0, across[4], jnp.where(sub == 3, across[5], 0.0))
    both_y = jnp.concatenate([jnp.broadcast_to(across[f], (8, 128)) for f in (2, 3)], axis=0)
    from_z = (face_z.reshape(40, 8, 128) * both_z[None]).reshape(WIDTH, 128)
    from_y = (face_y.reshape(20, 16, 128) * both_y[None]).reshape(WIDTH, 128)
    return jnp.sum(part + (from_z + from_y), axis=1, keepdims=True)


def gram_column(basis, k):
    chains = []
    for tile in range(3):
        total, low = None, None
        for e in range(ELEM_DEV):
            x = basis[e, :, 128 * tile : 128 * tile + 128]
            b = jnp.broadcast_to(basis[e, k : k + 1, 128 * tile : 128 * tile + 128], (8, 128))
            p, err = two_prod(x, b)
            if total is None:
                total, low = p, err
            else:
                total, more = two_sum(total, p)
                low = low + (err + more)
        chains.append((total, low))
    total, low = chains[0]
    for other, other_low in chains[1:]:
        total, more = two_sum(total, other)
        low = low + (other_low + more)
    grid = jnp.minimum(256.0 * jnp.max(jnp.abs(total), axis=1, keepdims=True), 1e38)
    lead = (total + grid) - grid
    rest = (total - lead) + low
    return jnp.sum(lead, axis=1, keepdims=True), jnp.sum(rest, axis=1, keepdims=True)


def pack(message, k, pair):
    lane = iota((8, 128), 1)
    message = jnp.where(lane == k, pair[0], message)
    return jnp.where(lane == 8 + k, pair[1], message)


def sum_messages(tiles):
    chains = []
    for start in range(8):
        mine = tiles[start::8]
        total, low = mine[0], jnp.zeros((8, 128), F32)
        for tile in mine[1:]:
            total, more = two_sum(total, tile)
            low = low + more
        chains.append((total, low))
    while len(chains) > 1:
        merged = []
        for a, b in zip(chains[::2], chains[1::2]):
            total, more = two_sum(a[0], b[0])
            merged.append((total, (a[1] + b[1]) + more))
        chains = merged
    total, low = chains[0]
    return fast_two_sum(total, low + pltpu.roll(total, 120, 1))


def repack(high, low):
    return jnp.where(iota((8, 128), 1) < 8, high, pltpu.roll(low, 8, 1))


def solve(high, low):
    def spread(tile, i, k):
        return jnp.broadcast_to(tile[i : i + 1, k : k + 1], (8, 128))

    g = {(i, k): (spread(high, i, k), spread(low, i, k)) for i in range(BASIS) for k in range(i, BASIS)}
    factors, inverse, r = {}, [], {}
    for j in range(BASIS):
        d, d_low = g[j, j]
        root = lax.rsqrt(d)
        root = root * (1.5 - 0.5 * d * root * root)
        inverse.append(root)
        for k in range(j, BASIS):
            r[j, k] = g[j, k][0] * root
        if j == BASIS - 1:
            break
        recip = 1.0 / d
        ls = {}
        for i in range(j + 1, BASIS):
            t, t_low = g[j, i]
            first = t * recip
            p, err = two_prod(first, d)
            rest = (((t - p) - err) + t_low) - first * d_low
            ls[i] = fast_two_sum(first, rest * recip)
            factors[i, j] = ls[i][0]
        for i in range(j + 1, BASIS):
            for k in range(i, BASIS):
                t, t_low = g[j, k]
                p, err = two_prod(ls[i][0], t)
                err = err + (ls[i][0] * t_low + ls[i][1] * t)
                total, more = two_sum(g[i, k][0], -p)
                g[i, k] = fast_two_sum(total, more + (g[i, k][1] - err))
    h = {}
    for j in range(POWERS):
        for i in range(j + 2):
            value = r[i, j + 1]
            for m in range(max(i - 1, 0), j):
                value = value - h[i, m] * r[m, j]
            h[i, j] = value * inverse[j]
    normal = {}
    for a in range(POWERS):
        for b in range(a, POWERS):
            value = h[0, a] * h[0, b]
            for i in range(1, a + 2):
                value = value + h[i, a] * h[i, b]
            normal[a, b] = value
    target = [r[0, 0] * h[0, a] for a in range(POWERS)]
    lower, recips = {}, []
    for j in range(POWERS):
        recips.append(1.0 / normal[j, j])
        for i in range(j + 1, POWERS):
            lower[i, j] = normal[j, i] * recips[j]
        for i in range(j + 1, POWERS):
            target[i] = target[i] - lower[i, j] * target[j]
            for k in range(i, POWERS):
                normal[i, k] = normal[i, k] - lower[i, j] * normal[j, k]
    y = [target[j] * recips[j] for j in range(POWERS)]
    for j in range(POWERS - 1, -1, -1):
        for i in range(j + 1, POWERS):
            y[j] = y[j] - lower[i, j] * y[i]
    return factors, r, inverse, y


def kernel(
    nb_hbm, rhs_hbm, diag_hbm, face_hbm,
    basis, gram,
    nb_ref, rhs_ref, diag, face, face_y, face_z, rows, traces, out_x, in_a, in_b, in_c, in_d, packed_face, far, message, got_plane, got_z,
    load_sem, far_send, far_recv, x_send, x_recv, p_send, p_recv, z_send, z_recv, ready,
):
    in_x = ((in_a, in_b), (in_c, in_d))
    me = lax.axis_index("elem")
    place, z, core = me % PLANE, me // PLANE, me % 2
    plane0 = me - place

    loads = [
        pltpu.make_async_copy(rhs_hbm, rhs_ref, load_sem.at[2]),
        pltpu.make_async_copy(diag_hbm, diag, load_sem.at[0]),
        pltpu.make_async_copy(face_hbm, face, load_sem.at[1]),
        pltpu.make_async_copy(nb_hbm, nb_ref, load_sem.at[3]),
    ]
    barrier = pltpu.get_barrier_semaphore()

    def greet(device):
        pl.semaphore_signal(barrier, inc=1, device_id=(device,), device_id_type=MESH)

    def other_plane(d, to):
        return ((z + d) % N_Z) * PLANE + place - core + to

    @pl.when(core == 1)
    def _():
        greet(plane0 + (place + PLANE - 1) % PLANE)
        greet(plane0 + (place + 1) % PLANE)

        @pl.when(jnp.logical_and(place == PLANE - 1, me < N_DEV - 1))
        def _():
            greet(me + 1)

    @pl.when(core == 0)
    def _():
        @pl.when(me > 0)
        def _():
            greet(me - 1)

        greet(me + 1)

    for load in loads:
        load.start()

    @pl.when(core == 1)
    def _():
        for d in range(2, PLANE - 1):
            greet(plane0 + (place + d) % PLANE)

    greet(other_plane(1, 1))
    greet(other_plane(N_Z - 1, 1))

    def tell(reach):
        @pl.when(core == 1)
        def _():
            for d in (reach, N_Z - reach):
                pl.semaphore_signal(
                    ready.at[reach // 2], inc=1, device_id=(other_plane(d, 1),), device_id_type=MESH
                )

    def hear(reach):
        @pl.when(core == 1)
        def _():
            pl.semaphore_wait(ready.at[reach // 2], 2)

    basis[...] = jnp.zeros(basis.shape, F32)
    face_y[...] = jnp.zeros(face_y.shape, F32)
    face_z[...] = jnp.zeros(face_z.shape, F32)
    rows[...] = jnp.zeros(rows.shape, F32)
    loads[0].wait()
    rows[0:ELEM_DEV, 0:WIDTH] = rhs_ref[...]

    def store_row(k, e, tiles):
        for t in range(3):
            lanes = min(128, WIDTH - 128 * t)
            row = jnp.sum(tiles[t], axis=0, keepdims=True)[:, :lanes]
            basis[e, k : k + 1, 128 * t : 128 * t + lanes] = row
            rows[e : e + 1, 128 * t : 128 * t + lanes] = row

    def make_traces():
        got = trace_tiles([rows[:, 128 * t : 128 * t + 128] for t in range(3)])
        for f in range(6):
            traces[f] = got[f]

    for e in range(ELEM_DEV):
        basis[e, 0:1, 0:WIDTH] = rhs_ref[e : e + 1, :]
    make_traces()

    def x_traces(tiles):
        got = trace_tiles(tiles)
        return got[0], got[1]

    def send_x(step, kind):
        for side in range(2):
            @pl.when(me > 0 if side == 0 else me < N_DEV - 1)
            def _():
                x_copy(step, kind, side).start()

    def x_copy(step, kind, side):
        return pltpu.make_async_remote_copy(
            src_ref=out_x.at[step, kind, side],
            dst_ref=in_x[step][kind].at[1 - side],
            send_sem=x_send.at[step, kind, side],
            recv_sem=x_recv.at[step, kind, 1 - side],
            device_id=(me - 1 if side == 0 else me + 1,),
            device_id_type=MESH,
        )

    def wait_x(step, kind):
        for side in range(2):
            @pl.when(me < N_DEV - 1 if side == 0 else me > 0)
            def _():
                x_copy(step, kind, side).wait_recv()

    def far_copy(side):
        return pltpu.make_async_remote_copy(
            src_ref=packed_face.at[side],
            dst_ref=far.at[1 - side, pl.ds(0, 3)],
            send_sem=far_send.at[side],
            recv_sem=far_recv.at[1 - side],
            device_id=(me - 1 if side == 0 else me + 1,),
            device_id_type=MESH,
        )

    out_x[0, 0, 0] = traces[0]
    out_x[0, 0, 1] = traces[1]
    loads[2].wait()
    for side in range(2):
        packed_face[side, 2, :, FACE_WIDTH:128] = jnp.zeros((FACE_WIDTH, 48), F32)
        for b in range(3):
            packed_face[side, b, :, 0:FACE_WIDTH] = face[b, side]
        packed_face[side, 0, :, FACE_WIDTH:128] = face[3, side, :, 0:48]
        packed_face[side, 1, :, FACE_WIDTH:128] = jnp.concatenate(
            [face[3, side, :, 48:FACE_WIDTH], jnp.zeros((FACE_WIDTH, 16), F32)], axis=1
        )
    for e in range(ELEM_DEV):
        for c in range(20):
            face_y[e, 16 * c : 16 * c + 4, 0:FACE_WIDTH] = face[e, 2, 4 * c : 4 * c + 4, :]
            face_y[e, 16 * c + 12 : 16 * c + 16, 0:FACE_WIDTH] = face[e, 3, 4 * c : 4 * c + 4, :]
        for f, k in ((4, 0), (5, 3)):
            face_z[e, pl.ds(k, FACE_WIDTH, stride=4), :] = jnp.concatenate(
                [face[e, f], jnp.zeros((FACE_WIDTH, 128 - FACE_WIDTH), F32)], axis=1
            )
    loads[1].wait()
    loads[3].wait()

    base = me * ELEM_DEV

    def link(e, f):
        wanted = nb_ref[e, f]
        first = base + (-ELEM_DEV if f == 0 else ELEM_DEV if f == 1 else 0)
        return wanted >= 0, jnp.clip(wanted - first, 0, ELEM_DEV - 1)

    links = [[link(e, f) for f in range(6)] for e in range(ELEM_DEV)]

    def own_part(out):
        for e in range(ELEM_DEV):
            across = {}
            for f in range(2, 6):
                valid, index = links[e][f]
                across[f] = jnp.where(valid, traces[f ^ 1, pl.ds(index, 1), :], 0.0)
            out.append(place_element(own_column(diag[e], face_y[e], face_z[e], rows[e : e + 1, :], across)))

    def x_part(e, across):
        total = None
        for f in range(2):
            part = place_face(f, matvec(face[e, f], across[f][:, 0:FACE_WIDTH]))
            total = part if total is None else add_all(total, part)
        return total

    def received(step, kind, e, f):
        valid, index = links[e][f]
        return valid, in_x[step][kind][f, pl.ds(index, 1), :]

    heard = jnp.where(
        core == 1,
        4 + 15 + 2 - jnp.where(me == N_DEV - 1, 1, 0),
        16 + jnp.where(jnp.logical_and(place == 0, me > 0), 1, 0),
    )
    grams = {}
    for step in range(2):
        k = 2 * step
        own = []
        own_part(own)
        sums = [
            jnp.concatenate([jnp.sum(own[e][t], axis=0, keepdims=True) for e in range(ELEM_DEV)] * 2, axis=0)
            for t in range(3)
        ]
        low, high = x_traces(sums)
        out_x[step, 1, 0] = low
        out_x[step, 1, 1] = high
        if step == 0:
            pl.semaphore_wait(barrier, heard)
            send_x(0, 0)
            send_x(0, 1)
            for side in range(2):
                @pl.when(me > 0 if side == 0 else me < N_DEV - 1)
                def _():
                    far_copy(side).start()
            tell(1)
        else:
            send_x(step, 1)
        kept = [[traces[f, e : e + 1, 0:FACE_WIDTH] for f in range(2)] for e in range(ELEM_DEV)]

        def added(e, f):
            return place_trace(matvec(far[f, links[e][f][1], :, 0:FACE_WIDTH], kept[e][f]))

        if step == 1:
            back = [[added(e, f) for f in range(2)] for e in range(ELEM_DEV)]
        if step == 1:
            for kk in range(3):
                grams[kk] = gram_column(basis, kk)
        wait_x(step, 0)
        hear(1 + step)
        tell(2 + 2 * step)
        for e in range(ELEM_DEV):
            across = []
            for f in range(2):
                valid, row = received(step, 0, e, f)
                across.append(jnp.where(valid, row, 0.0))
            store_row(k + 1, e, add_all(own[e], x_part(e, across)))
        make_traces()
        own = []
        own_part(own)
        wait_x(step, 1)
        if step == 0:
            for side in range(2):
                @pl.when(me < N_DEV - 1 if side == 0 else me > 0)
                def _():
                    far_copy(side).wait_recv()
                head = far[1 - side, 0:2, :, FACE_WIDTH:128]
                far[1 - side, 3, :, 0:48] = head[0]
                far[1 - side, 3, :, 48:FACE_WIDTH] = head[1, :, 0:32]
            back = [[added(e, f) for f in range(2)] for e in range(ELEM_DEV)]
        for e in range(ELEM_DEV):
            across = []
            for f in range(2):
                valid, row = received(step, 1, e, f)
                across.append(jnp.where(valid, row + back[e][f], 0.0))
            store_row(k + 2, e, add_all(own[e], x_part(e, across)))
        if step == 0:
            make_traces()
            out_x[1, 0, 0] = traces[0]
            out_x[1, 0, 1] = traces[1]
            send_x(1, 0)

    grams[3] = gram_column(basis, 3)
    grams[4] = gram_column(basis, 4)
    packed = jnp.zeros((8, 128), F32)
    for k in range(BASIS):
        packed = pack(packed, k, grams[k])
    message[0] = packed

    def plane_copy(d):
        return pltpu.make_async_remote_copy(
            src_ref=message.at[0],
            dst_ref=got_plane.at[PLANE - d - 1],
            send_sem=p_send,
            recv_sem=p_recv,
            device_id=(plane0 + (place + d) % PLANE,),
            device_id_type=MESH,
        )

    def z_copy(source, plane, to, same):
        return pltpu.make_async_remote_copy(
            src_ref=message.at[source],
            dst_ref=got_z.at[(z - plane + N_Z) % N_Z + (0 if same else N_Z)],
            send_sem=z_send,
            recv_sem=z_recv,
            device_id=(plane * PLANE + place - core + to,),
            device_id_type=MESH,
        )

    def send_z(source, mine):
        for i in range(N_Z - 1):
            plane = i + jnp.where(z <= i, 1, 0)
            z_copy(source, plane, 1, mine == 1).start()
            z_copy(source, plane, 0, mine == 0).start()
        z_copy(source, z, 1 - mine, False).start()
        got_z[0] = message[source]

    def wait_all(ref, sem):
        pltpu.make_async_copy(ref, ref, sem).wait()

    @pl.when(core == 1)
    def _():
        for d in range(2, PLANE, 2):
            plane_copy(d).start()
        hear(4)
        pl.semaphore_signal(ready.at[3], inc=1, device_id=(me - 1,), device_id_type=MESH)
        wait_all(got_plane, p_recv)
        high, low = sum_messages([message[0]] + [got_plane[i] for i in range(PLANE - 2)])
        message[1] = repack(high, low)
        send_z(1, 1)

    @pl.when(core == 0)
    def _():
        for d in range(3, PLANE, 2):
            plane_copy(d).start()
        pl.semaphore_wait(ready.at[3], 1)
        send_z(0, 0)

    wait_all(got_z.at[pl.ds(1, 2 * N_Z - 1)], z_recv)
    high, low = sum_messages([got_z[i] for i in range(2 * N_Z)])
    gram[0] = high
    gram[1] = low

    for side in range(2):
        @pl.when(me > 0 if side == 0 else me < N_DEV - 1)
        def _():
            far_copy(side).wait_send()
            for step in range(2):
                for kind in range(2):
                    x_copy(step, kind, side).wait_send()

    wait_all(got_plane.at[pl.ds(0, 15)], p_send)
    wait_all(got_z.at[pl.ds(1, 2 * N_Z - 1)], z_send)


def finish(basis_ref, gram_ref, q_hbm, r_hbm, up_hbm, q_ref, r_ref, up_ref, sem):
    stores = [
        pltpu.make_async_copy(q_ref, q_hbm, sem.at[0]),
        pltpu.make_async_copy(r_ref, r_hbm, sem.at[1]),
        pltpu.make_async_copy(up_ref, up_hbm, sem.at[2]),
    ]
    high, low = gram_ref[0], gram_ref[1]
    factors, r, inverse, y = solve(high, low)

    sub, lane = iota((8, 128), 0), iota((8, 128), 1)
    r_tile = jnp.zeros((8, 128), F32)
    for (i, k), value in r.items():
        r_tile = jnp.where(jnp.logical_and(sub == i, lane == k), value, r_tile)
    r_ref[...] = r_tile[0:BASIS, 0:BASIS]
    stores[1].start()
    columns = []
    for j in range(BASIS - 1):
        column = jnp.zeros((8, 128), F32)
        for i in range(j + 1, BASIS):
            column = jnp.where(sub == i, factors[i, j], column)
        columns.append(column)
    scale, weight = jnp.zeros((8, 128), F32), jnp.zeros((8, 128), F32)
    for j in range(BASIS):
        scale = jnp.where(sub == j, inverse[j], scale)
        if j < POWERS:
            weight = jnp.where(sub == j, y[j], weight)
    for e in range(ELEM_DEV):
        for t in range(3):
            lanes = min(128, WIDTH - 128 * t)
            x = basis_ref[e, :, 128 * t : 128 * t + 128]
            for j in range(BASIS - 1):
                x = x - columns[j] * x[j : j + 1, :]
            x = x * scale
            q_ref[:, e, 128 * t : 128 * t + lanes] = x[0:BASIS, 0:lanes]
            update = jnp.sum(x * weight, axis=0, keepdims=True)
            up_ref[e : e + 1, 128 * t : 128 * t + lanes] = update[:, 0:lanes]
    stores[0].start()
    stores[2].start()
    for store in stores:
        store.wait()


def body(right_side, diag_blocks, face_blocks, neighbours):
    hbm = pl.BlockSpec(memory_space=pl.ANY)
    vmem = pl.BlockSpec(memory_space=pltpu.VMEM)
    tile = (8, 128)
    operands = [
        pltpu.with_memory_space_constraint(x, pltpu.HBM)
        for x in (neighbours, right_side, diag_blocks, face_blocks)
    ]
    basis, gram = pl.pallas_call(
        kernel,
        out_shape=(
            pltpu.VMEM((ELEM_DEV, 8, 384), F32),
            pltpu.VMEM((2,) + tile, F32),
        ),
        in_specs=[hbm] * 4,
        out_specs=(vmem, vmem),
        scratch_shapes=[
            pltpu.SMEM((ELEM_DEV, 6), jnp.int32),
            pltpu.VMEM((ELEM_DEV, WIDTH), F32),
            pltpu.VMEM((ELEM_DEV, WIDTH, WIDTH), F32),
            pltpu.VMEM((ELEM_DEV, 6, FACE_WIDTH, FACE_WIDTH), F32),
            pltpu.VMEM((ELEM_DEV, WIDTH, 128), F32),
            pltpu.VMEM((ELEM_DEV, WIDTH, 128), F32),
            pltpu.VMEM((8, 384), F32),
            pltpu.VMEM((6,) + tile, F32),
            pltpu.VMEM((2, 2, 2) + tile, F32),
            pltpu.VMEM((2,) + tile, F32),
            pltpu.VMEM((2,) + tile, F32),
            pltpu.VMEM((2,) + tile, F32),
            pltpu.VMEM((2,) + tile, F32),
            pltpu.VMEM((2, 3, FACE_WIDTH, 128), F32),
            pltpu.VMEM((2, ELEM_DEV, FACE_WIDTH, 128), F32),
            pltpu.VMEM((2,) + tile, F32),
            pltpu.VMEM((PLANE - 2,) + tile, F32),
            pltpu.VMEM((2 * N_Z,) + tile, F32),
            pltpu.SemaphoreType.DMA((4,)),
            pltpu.SemaphoreType.DMA((2,)),
            pltpu.SemaphoreType.DMA((2,)),
            pltpu.SemaphoreType.DMA((2, 2, 2)),
            pltpu.SemaphoreType.DMA((2, 2, 2)),
            pltpu.SemaphoreType.DMA,
            pltpu.SemaphoreType.DMA,
            pltpu.SemaphoreType.DMA,
            pltpu.SemaphoreType.DMA,
            pltpu.SemaphoreType.REGULAR((4,)),
        ],
        compiler_params=pltpu.CompilerParams(
            collective_id=0, has_side_effects=True, vmem_limit_bytes=24 * 2**20
        ),
    )(*operands)
    basis_q, r_factor, update = pl.pallas_call(
        finish,
        out_shape=(
            jax.ShapeDtypeStruct((BASIS, ELEM_DEV, WIDTH), F32),
            jax.ShapeDtypeStruct((BASIS, BASIS), F32),
            jax.ShapeDtypeStruct((ELEM_DEV, WIDTH), F32),
        ),
        in_specs=[vmem, vmem],
        out_specs=(hbm, hbm, hbm),
        scratch_shapes=[
            pltpu.VMEM((BASIS, ELEM_DEV, WIDTH), F32),
            pltpu.VMEM((BASIS, BASIS), F32),
            pltpu.VMEM((ELEM_DEV, WIDTH), F32),
            pltpu.SemaphoreType.DMA((3,)),
        ],
        compiler_params=pltpu.CompilerParams(vmem_limit_bytes=4 * 2**20),
    )(basis, gram)
    return basis_q.transpose(1, 0, 2), r_factor, update


def solution(mesh):
    in_specs = (
        P("elem", None),
        P("elem", None, None),
        P("elem", None, None, None),
        P("elem", None),
    )
    out_specs = (P("elem", None, None), P(), P("elem", None))
    return jax.shard_map(body, mesh=mesh, in_specs=in_specs, out_specs=out_specs, check_vma=False)
```
